32 devices in a mesh: seq: 8 (over z, y), head: 4 (over x, core).
Axes of the slice: x: 2, y: 2, z: 4, core: 2. Of those that a mesh axis runs over, the one named last changes fastest.
Arguments:
- query_one: bfloat16 [8, 2048, 128], P('head', 'seq'), may hold values from -0.5 to 0.5
- key_one: bfloat16 [8, 2048, 128], P('head', 'seq'), may hold values from -6 to 6
- value_one: bfloat16 [8, 2048, 128], P('head', 'seq'), may hold values from -6 to 6
- decay_one: float32 [8, 2048], P('head', 'seq'), may hold values from -1 to 0
- initial_one: float32 [8, 128, 128], P('head'), may hold values from -256 to 256
- query_two: bfloat16 [8, 2048, 128], P('head', 'seq'), may hold values from -0.5 to 0.5
- key_two: bfloat16 [8, 2048, 128], P('head', 'seq'), may hold values from -6 to 6
- decay_two: float32 [8, 2048], P('head', 'seq'), may hold values from -1 to 0
- initial_two: float32 [8, 128, 128], P('head'), may hold values from -256 to 256
- grad_out: bfloat16 [8, 2048, 128], P('head', 'seq'), may hold values from -6 to 6
Outputs:
- output: bfloat16 [8, 2048, 128], P('head', 'seq')
- grad_query_one: bfloat16 [8, 2048, 128], P('head', 'seq')
- grad_key_one: bfloat16 [8, 2048, 128], P('head', 'seq')
- grad_value_one: bfloat16 [8, 2048, 128], P('head', 'seq')
- grad_query_two: bfloat16 [8, 2048, 128], P('head', 'seq')
- grad_key_two: bfloat16 [8, 2048, 128], P('head', 'seq')
The draws below stay inside these ranges and needn't reach their ends.
All inputs are finite; a program needn't handle non-finite values.
Results may differ from the reference program's by a relative error of at most 0.015.
Values sent between devices are 32-bit elements; how exact they have to be, the bound alone decides.
A program may use at most 64 MiB of HBM per device.

```python
import math
import jax
import jax.numpy as jnp
from jax import lax

DH = 128
SPAN = 256
TOK_DEV = 256
SEQUENCE_TOKENS = 2048
GROUP_HEADS = 8


def decay_law(key):
    random_subkeys = jax.random.split(key, 7)
    ranking = jax.random.permutation(random_subkeys[0], GROUP_HEADS)
    keep_count = GROUP_HEADS // 2
    slow_heads = (ranking < keep_count)[:, None]
    slow_rate = jnp.exp(jax.random.uniform(random_subkeys[1], (GROUP_HEADS, 1), jnp.float32, math.log(0.2), 0.0)) / SEQUENCE_TOKENS
    fast_rate = jnp.exp(jax.random.uniform(random_subkeys[2], (GROUP_HEADS, 1), jnp.float32, math.log(1.0 / 50.0), math.log(1.0 / 30.0)))
    baseline_decay_rate = jnp.where(slow_heads, slow_rate, fast_rate)
    blocks = SEQUENCE_TOKENS // TOK_DEV
    device_multiplier = jnp.exp(jax.random.uniform(random_subkeys[3], (GROUP_HEADS, blocks), jnp.float32, math.log(0.5), math.log(2.0)))
    device_multiplier = jnp.repeat(device_multiplier, TOK_DEV, axis=1)
    jitter_amplitude = jax.random.uniform(random_subkeys[4], (GROUP_HEADS, SEQUENCE_TOKENS), jnp.float32, 0.5, 1.5)
    token_positions = jnp.arange(SEQUENCE_TOKENS)
    spike_position = jax.random.randint(random_subkeys[5], (GROUP_HEADS, 3, 1), 0, SEQUENCE_TOKENS)
    spike_length = jax.random.uniform(random_subkeys[6], (GROUP_HEADS, 3, 1), jnp.float32, 0.22, 0.4)
    spike_penalty = jnp.sum(jnp.where(token_positions[None, None, :] == spike_position, spike_length, 0.0), axis=1)
    return (-(baseline_decay_rate * device_multiplier * jitter_amplitude) - spike_penalty).astype(jnp.float32)


def draw_decay_one(key, part):
    return decay_law(jax.random.fold_in(key, 11))


def draw_decay_two(key, part):
    return decay_law(jax.random.fold_in(key, 23))


def levels(key, dims, shards, low, largest):
    factor_of, own = 1.0, jax.random.fold_in(key, 6)
    for dim, blocks in shards:
        steps = jnp.exp(jax.random.uniform(jax.random.fold_in(own, dim), (blocks,), jnp.float32, low / len(shards), largest / len(shards)))
        factor_of = factor_of * jnp.repeat(steps, dims[dim] // blocks).reshape([-1 if axis == dim else 1 for axis in range(len(dims))])
    return factor_of


def centred(rng, shape, deviation, reach, pieces=(), held_as=jnp.bfloat16):
    level = levels(rng, shape, pieces, -0.22, 0.18) if pieces else 1.0
    result = jax.random.normal(rng, shape, jnp.float32) * deviation * level
    return jnp.minimum(jnp.maximum(result, -reach), reach).astype(held_as)


def setup_inputs(seed: int = 0) -> dict:
    key_of = jax.random.split(jax.random.key(seed), 11)
    query_one = centred(key_of[0], (GROUP_HEADS, SEQUENCE_TOKENS, DH), (DH ** -0.5), 0.5, ((0, 4), (1, 8)))
    key_one = centred(key_of[1], (GROUP_HEADS, SEQUENCE_TOKENS, DH), 1.0, 6.0, ((0, 4), (1, 8)))
    value_one = centred(key_of[2], (GROUP_HEADS, SEQUENCE_TOKENS, DH), 1.0, 6.0, ((0, 4), (1, 8)))
    decay_one = draw_decay_one(jax.random.fold_in(key_of[10], 71), 0)
    initial_one = centred(key_of[4], (GROUP_HEADS, DH, DH), (SEQUENCE_TOKENS ** 0.5), 256.0, ((0, 4),), jnp.float32)
    query_two = centred(key_of[5], (GROUP_HEADS, SEQUENCE_TOKENS, DH), (DH ** -0.5), 0.5, ((0, 4), (1, 8)))
    key_two = centred(key_of[6], (GROUP_HEADS, SEQUENCE_TOKENS, DH), 1.0, 6.0, ((0, 4), (1, 8)))
    decay_two = draw_decay_two(jax.random.fold_in(key_of[10], 71), 0)
    initial_two = centred(key_of[8], (GROUP_HEADS, DH, DH), (SEQUENCE_TOKENS ** 0.5), 256.0, ((0, 4),), jnp.float32)
    grad_out = centred(key_of[9], (GROUP_HEADS, SEQUENCE_TOKENS, DH), 1.0, 6.0, ((0, 4), (1, 8)))
    return dict(query_one=query_one, key_one=key_one, value_one=value_one, decay_one=decay_one, initial_one=initial_one, query_two=query_two, key_two=key_two, decay_two=decay_two, initial_two=initial_two, grad_out=grad_out)


def rounded(array):
    return lax.optimization_barrier(array.astype(jnp.bfloat16)).astype(jnp.float32)

def masked_exp(diff, keep_mask):
    return jnp.where(keep_mask, jnp.exp(jnp.where(keep_mask, diff, 0.0)), 0.0)

def to_blocks(array, head_count, span_count):
    shaped = array.reshape((head_count, span_count, SPAN) + array.shape[2:])
    return jnp.moveaxis(shaped, 1, 0)

def from_blocks(array):
    moved = jnp.moveaxis(array, 0, 1)
    return moved.reshape((moved.shape[0], moved.shape[1] * moved.shape[2]) + moved.shape[3:])

def forward_layer(queries, keys_block, values, log_decay, initial):
    head_count, total_len, feature_dim = queries.shape
    span_count = total_len // SPAN
    within = jnp.cumsum(to_blocks(log_decay, head_count, span_count), axis=2)
    offsets = jnp.arange(SPAN)
    causal = (offsets[None, :] <= offsets[:, None])[None]

    def step(running, inputs):
        query_blk, key_blk, value_blk, within_blk = inputs
        query_f = query_blk.astype(jnp.float32)
        key_f = key_blk.astype(jnp.float32)
        value_f = value_blk.astype(jnp.float32)
        decay_mask = masked_exp(within_blk[:, :, None] - within_blk[:, None, :], causal)
        scores = jnp.einsum('hcd,hsd->hcs', query_f, key_f)
        weights = rounded(scores * decay_mask)
        states_low = rounded(running)
        output = jnp.einsum('hcs,hse->hce', weights, value_f)
        output = output + jnp.exp(within_blk)[:, :, None] * jnp.einsum('hcd,hde->hce', query_f, states_low)
        block_end = within_blk[:, -1]
        keys_scaled = rounded(key_f * jnp.exp(block_end[:, None] - within_blk)[:, :, None])
        updated = jnp.exp(block_end)[:, None, None] * running + jnp.einsum('hcd,hce->hde', keys_scaled, value_f)
        return (updated, (output, states_low))
    start = initial.astype(jnp.float32)
    inputs = (to_blocks(queries, head_count, span_count), to_blocks(keys_block, head_count, span_count), to_blocks(values, head_count, span_count), within)
    _, (outputs, states) = lax.scan(step, start, inputs)
    return (from_blocks(outputs), states)

def norm_of(output):
    return 1.0 / jnp.sqrt(lax.optimization_barrier(jnp.mean(output * output, axis=(0, 2))) + 1e-06)

def backward_layer(queries, keys_block, values, log_decay, output, norm_factor, states, grad_in):
    head_count, total_len, feature_dim = queries.shape
    span_count = total_len // SPAN
    normalized = output * norm_factor[None, :, None]
    cotangent = grad_in.astype(jnp.float32)
    inner_sum = lax.optimization_barrier(jnp.mean(cotangent * normalized, axis=(0, 2)))
    grad_core = rounded(norm_factor[None, :, None] * (cotangent - normalized * inner_sum[None, :, None]))
    within = jnp.cumsum(to_blocks(log_decay, head_count, span_count), axis=2)
    offsets = jnp.arange(SPAN)
    causal = (offsets[None, :] <= offsets[:, None])[None]

    def step(running, inputs):
        query_blk, key_blk, value_blk, within_blk, grad_blk, state_blk = inputs
        query_f = query_blk.astype(jnp.float32)
        key_f = key_blk.astype(jnp.float32)
        value_f = value_blk.astype(jnp.float32)
        grads_low = rounded(running)
        decay_mask = masked_exp(within_blk[:, :, None] - within_blk[:, None, :], causal)
        weights = rounded(jnp.einsum('hcd,hsd->hcs', query_f, key_f) * decay_mask)
        grad_scores = rounded(jnp.einsum('hce,hse->hcs', grad_blk, value_f) * decay_mask)
        grad_query = jnp.einsum('hcs,hsd->hcd', grad_scores, key_f)
        grad_query = grad_query + jnp.exp(within_blk)[:, :, None] * jnp.einsum('hce,hde->hcd', grad_blk, state_blk)
        block_end = within_blk[:, -1]
        tail_weight = jnp.exp(block_end[:, None] - within_blk)[:, :, None]
        grad_key = jnp.einsum('hcs,hcd->hsd', grad_scores, query_f)
        grad_key = grad_key + tail_weight * jnp.einsum('hse,hde->hsd', value_f, grads_low)
        grad_value = jnp.einsum('hcs,hce->hse', weights, grad_blk)
        grad_value = grad_value + tail_weight * jnp.einsum('hsd,hde->hse', key_f, grads_low)
        queries_scaled = rounded(query_f * jnp.exp(within_blk)[:, :, None])
        updated = jnp.exp(block_end)[:, None, None] * running + jnp.einsum('hcd,hce->hde', queries_scaled, grad_blk)
        return (updated, (grad_query, grad_key, grad_value))
    start = jnp.zeros((head_count, feature_dim, feature_dim), jnp.float32)
    inputs = (to_blocks(queries, head_count, span_count), to_blocks(keys_block, head_count, span_count), to_blocks(values, head_count, span_count), within, to_blocks(grad_core, head_count, span_count), states)
    _, (grad_query, grad_key, grad_value) = lax.scan(step, start, inputs, reverse=True)
    return (from_blocks(grad_query).astype(jnp.bfloat16), from_blocks(grad_key).astype(jnp.bfloat16), from_blocks(grad_value).astype(jnp.bfloat16))

def reference(query_one, key_one, value_one, decay_one, initial_one, query_two, key_two, decay_two, initial_two, grad_out):
    output_one, states_one = forward_layer(query_one, key_one, value_one, decay_one, initial_one)
    factor_one = norm_of(output_one)
    value_two = (output_one * factor_one[None, :, None]).astype(jnp.bfloat16)
    output_two, states_two = forward_layer(query_two, key_two, value_two, decay_two, initial_two)
    factor_two = norm_of(output_two)
    output = (output_two * factor_two[None, :, None]).astype(jnp.bfloat16)
    grads_two = backward_layer(query_two, key_two, value_two, decay_two, output_two, factor_two, states_two, grad_out)
    grads_one = backward_layer(query_one, key_one, value_one, decay_one, output_one, factor_one, states_one, grads_two[2])
    return (output, grads_one[0], grads_one[1], grads_one[2], grads_two[0], grads_two[1])
```

```python
import functools

import jax
import jax.numpy as jnp
from jax import lax
from jax.experimental import pallas as pl
from jax.experimental.pallas import tpu as pltpu
from jax.sharding import PartitionSpec as P

F32 = jnp.float32
BF16 = jnp.bfloat16
MESH = pl.DeviceIdType.MESH
EXACT = lax.Precision.HIGHEST


def nn(a, b):
    return lax.dot_general(a, b, (((1,), (0,)), ((), ())), preferred_element_type=F32)


def nt(a, b):
    return lax.dot_general(a, b, (((1,), (1,)), ((), ())), preferred_element_type=F32)


def tn(a, b):
    return lax.dot_general(a, b, (((0,), (0,)), ((), ())), preferred_element_type=F32)


def kernel(
    n, hc,
    q1, k1, v1, d1, i1, q2, k2, d2, i2, go,
    res, gq1, gk1, gv1, gq2, gk2,
    dec, mask, wts, ew, tail, part, outs, ks2t, qst, st, v2, gc, cot1, gkp, gvp,
    dt_out, dt_in, sc_out, sc_in, pf_out, pf_in, nm_out, nm_in,
    dt_send, dt_recv, sc_send, sc_recv, pf_send, pf_recv, nm_send, nm_recv,
):
    heads, tok, dh = q1.shape
    per_head = n // heads
    r = dh // per_head
    me, hme = lax.axis_index("seq"), lax.axis_index("head")
    my_head = me // per_head

    def seq_copy(src, dst, send, recv, peer):
        return pltpu.make_async_remote_copy(
            src_ref=src, dst_ref=dst, send_sem=send, recv_sem=recv,
            device_id=(peer, hme), device_id_type=MESH,
        )

    def head_copy(src, dst, send, recv, peer):
        return pltpu.make_async_remote_copy(
            src_ref=src, dst_ref=dst, send_sem=send, recv_sem=recv,
            device_id=(me, peer), device_id_type=MESH,
        )

    def seq_peers(body):
        if n <= 16:
            for step in range(1, n):
                body(lax.rem(me + step, n))
        else:
            def wrapped(step, carry):
                body(lax.rem(me + step, n))
                return carry
            lax.fori_loop(1, n, wrapped, 0)

    def head_peers(body):
        for step in range(1, hc):
            body(lax.rem(hme + step, hc))

    barrier = pltpu.get_barrier_semaphore()
    seq_peers(lambda p: pl.semaphore_signal(barrier, inc=1, device_id=(p, hme), device_id_type=MESH))
    head_peers(lambda p: pl.semaphore_signal(barrier, inc=1, device_id=(me, p), device_id_type=MESH))

    dec[...] = jnp.zeros_like(dec)
    dec[0:heads] = d1[...]
    dec[heads:2 * heads] = d2[...]
    rows_t = lax.broadcasted_iota(jnp.int32, (tok, tok), 0)
    cols_t = lax.broadcasted_iota(jnp.int32, (tok, tok), 1)
    upper = (rows_t <= cols_t).astype(F32)
    within_row = lax.dot_general(
        dec[...], upper, (((1,), (0,)), ((), ())), preferred_element_type=F32, precision=EXACT
    )
    within_col = within_row.T
    causal = cols_t <= rows_t
    for c in range(2 * heads):
        col = jnp.broadcast_to(within_col[:, c:c + 1], (tok, dh))
        end = jnp.broadcast_to(within_col[tok - 1:tok, c:c + 1], (1, dh))
        ew[c] = jnp.exp(col)
        tail[c] = jnp.exp(end - col)
        dt_out[c:c + 1] = jnp.exp(end)
    dt_in[me] = dt_out[...]

    pl.semaphore_wait(barrier, n - 1 + hc - 1)
    seq_peers(lambda p: seq_copy(dt_out, dt_in.at[me], dt_send, dt_recv.at[me], p).start())

    def scatter(k, h, state):
        for a in range(per_head):
            p = h * per_head + a
            sc_out[k, p] = state[a * r:(a + 1) * r]

            @pl.when(p != me)
            def _():
                seq_copy(sc_out.at[k, p], sc_in.at[k, me], sc_send.at[k], sc_recv.at[k, me], p).start()

    def solve(k, first, core, backward):
        sc_in[k, me] = sc_out[k, me]

        def step(j, carry):
            pf_out[k, j] = carry

            @pl.when(j != me)
            def _():
                seq_copy(pf_out.at[k, j], pf_in.at[k, me], pf_send.at[k], pf_recv.at[k, me], j).start()
                seq_copy(sc_out.at[k, j], sc_in.at[k, j], sc_send.at[k], sc_recv.at[k, j], j).wait_recv()

            factor = dt_in[j, pl.ds(core * heads + my_head, 1), :]
            return factor * carry + sc_in[k, j]

        if n <= 16:
            carry = first
            for j in (range(n - 1, -1, -1) if backward else range(n)):
                carry = step(j, carry)
        else:
            lax.fori_loop(0, n, lambda s, c: step(n - 1 - s if backward else s, c), first)
        pf_in[k, me] = pf_out[k, me]

    def collect(k, h):
        for a in range(per_head):
            p = h * per_head + a

            @pl.when(p != me)
            def _():
                seq_copy(pf_out.at[k, p], pf_in.at[k, p], pf_send.at[k], pf_recv.at[k, p], p).wait_recv()

        return jnp.concatenate([pf_in[k, h * per_head + a] for a in range(per_head)], axis=0).astype(BF16)

    ones = jnp.ones((8, dh), F32)

    def row_sum(value):
        return lax.dot_general(
            ones, value, (((1,), (1,)), ((), ())), preferred_element_type=F32, precision=EXACT
        )

    def share(m, value):
        nm_out[m] = value
        nm_in[m, hme] = value
        head_peers(lambda p: head_copy(nm_out.at[m], nm_in.at[m, hme], nm_send.at[m], nm_recv.at[m, hme], p).start())

    def shared(m):
        head_peers(lambda p: head_copy(nm_out.at[m], nm_in.at[m, p], nm_send.at[m], nm_recv.at[m, p], p).wait_recv())
        total = nm_in[m, 0]
        for p in range(1, hc):
            total = total + nm_in[m, p]
        return (total * (1.0 / (hc * heads * dh))).T

    def make_weights(c, q, k):
        m = jnp.exp(jnp.where(causal, within_col[:, c:c + 1] - within_row[c:c + 1, :], -1e30))
        mask[c] = m
        wts[c] = (nt(q, k) * m).astype(BF16)

    for h in range(heads):
        scaled = (k1[h].astype(F32) * tail[h]).astype(BF16)
        scatter(0, h, tn(scaled, v1[h]))
    for h in range(heads):
        make_weights(h, q1[h], k1[h])
        part[h] = nn(wts[h], v1[h])
    seq_peers(lambda p: seq_copy(dt_out, dt_in.at[p], dt_send, dt_recv.at[p], p).wait_recv())
    solve(0, i1[me], 0, False)
    for h in range(heads):
        c = heads + h
        make_weights(c, q2[h], k2[h])
        ks2t[h] = (k2[h].astype(F32) * tail[c]).T.astype(BF16)
        qst[h] = (q1[h].astype(F32) * ew[h]).T.astype(BF16)
        qst[c] = (q2[h].astype(F32) * ew[c]).T.astype(BF16)
    squares = jnp.zeros((tok, dh), F32)
    for h in range(heads):
        st[h] = collect(0, h)
        value = part[h] + ew[h] * nn(q1[h], st[h])
        outs[h] = value
        squares = squares + value * value
    share(0, row_sum(squares))
    factor_one = lax.rsqrt(shared(0)[:, 0:1] + 1e-06)

    for h in range(heads):
        value = outs[h] * factor_one
        outs[h] = value
        v2[h] = value.astype(BF16)
        scatter(1, h, nn(ks2t[h], v2[h]))
    solve(1, i2[me], 1, False)
    for h in range(heads):
        part[heads + h] = nn(wts[heads + h], v2[h])
    squares = jnp.zeros((tok, dh), F32)
    dots = jnp.zeros((tok, dh), F32)
    for h in range(heads):
        c = heads + h
        st[c] = collect(1, h)
        value = part[c] + ew[c] * nn(q2[h], st[c])
        outs[c] = value
        squares = squares + value * value
        dots = dots + value * go[h].astype(F32)
    first_rows = lax.broadcasted_iota(jnp.int32, (8, tok), 0) < 4
    share(1, jnp.where(first_rows, row_sum(squares), row_sum(dots)))
    both = shared(1)
    factor_two = lax.rsqrt(both[:, 0:1] + 1e-06)
    inner_two = both[:, 4:5] * factor_two

    def backward(core, k, q_ref, k_ref, v_ref, gq_ref, grads):
        for h in range(heads):
            gc[h] = grads(h)
            scatter(k, h, nn(qst[core * heads + h], gc[h]))
        solve(k, jnp.zeros((r, dh), F32), core, True)
        for h in range(heads):
            c = core * heads + h
            gs = (nt(gc[h], v_ref[h]) * mask[c]).astype(BF16)
            gvp[h] = tn(wts[c], gc[h])
            gkp[h] = tn(gs, q_ref[h])
            gq_ref[h] = (nn(gs, k_ref[h]) + ew[c] * nt(gc[h], st[c])).astype(BF16)

    def grads_two(h):
        normalized = outs[heads + h] * factor_two
        res[h] = normalized.astype(BF16)
        return (factor_two * (go[h].astype(F32) - normalized * inner_two)).astype(BF16)

    backward(1, 2, q2, k2, v2, gq2, grads_two)
    dots = jnp.zeros((tok, dh), F32)
    leaving = []
    for h in range(heads):
        c = heads + h
        leaving.append(collect(2, h))
        cot1[h] = (gvp[h] + tail[c] * nn(k2[h], leaving[h])).astype(BF16)
        dots = dots + cot1[h].astype(F32) * outs[h]
    share(2, row_sum(dots))
    for h in range(heads):
        gk2[h] = (gkp[h] + tail[heads + h] * nt(v2[h], leaving[h])).astype(BF16)
    inner_one = shared(2)[:, 0:1]

    def grads_one(h):
        return (factor_one * (cot1[h].astype(F32) - outs[h] * inner_one)).astype(BF16)

    backward(0, 3, q1, k1, v1, gq1, grads_one)
    for h in range(heads):
        low = collect(3, h)
        gv1[h] = (gvp[h] + tail[h] * nn(k1[h], low)).astype(BF16)
        gk1[h] = (gkp[h] + tail[h] * nt(v1[h], low)).astype(BF16)

    def drain(ref, sem, count):
        block = ref.at[pl.ds(0, count)]
        seq_copy(block, block, sem, sem, lax.rem(me + 1, n)).wait_send()

    drain(dt_in, dt_send, n - 1)
    for k in range(4):
        drain(sc_out.at[k], sc_send.at[k], n - 1)
        drain(pf_out.at[k], pf_send.at[k], n - 1)
    for m in range(3):
        drain(nm_in.at[m], nm_send.at[m], hc - 1)


def local(n, hc, q1, k1, v1, d1, i1, q2, k2, d2, i2, go):
    heads, tok, dh = q1.shape
    r = heads * dh // n
    cores = 2 * heads
    pieces = (4, n, r, dh)
    vmem, dma = pltpu.VMEM, pltpu.SemaphoreType.DMA
    scratch = [
        vmem((8, tok), F32),
        vmem((cores, tok, tok), F32),
        vmem((cores, tok, tok), BF16),
        vmem((cores, tok, dh), F32),
        vmem((cores, tok, dh), F32),
        vmem((cores, tok, dh), F32),
        vmem((cores, tok, dh), F32),
        vmem((heads, dh, tok), BF16),
        vmem((cores, dh, tok), BF16),
        vmem((cores, dh, dh), BF16),
        vmem((heads, tok, dh), BF16),
        vmem((heads, tok, dh), BF16),
        vmem((heads, tok, dh), BF16),
        vmem((heads, tok, dh), F32),
        vmem((heads, tok, dh), F32),
        vmem((8, dh), F32),
        vmem((n, 8, dh), F32),
        vmem(pieces, F32), vmem(pieces, F32), vmem(pieces, F32), vmem(pieces, F32),
        vmem((3, 8, tok), F32),
        vmem((3, hc, 8, tok), F32),
        dma, dma((n,)), dma((4,)), dma((4, n)), dma((4,)), dma((4, n)), dma((3,)), dma((3, hc)),
    ]
    out = jax.ShapeDtypeStruct((heads, tok, dh), BF16)
    return pl.pallas_call(
        functools.partial(kernel, n, hc),
        out_shape=[out] * 6,
        in_specs=[pl.BlockSpec(memory_space=pltpu.VMEM)] * 10,
        out_specs=[pl.BlockSpec(memory_space=pltpu.VMEM)] * 6,
        scratch_shapes=scratch,
        compiler_params=pltpu.CompilerParams(
            collective_id=0, has_side_effects=True, vmem_limit_bytes=48 * 1024 * 1024
        ),
    )(q1, k1, v1, d1, i1.reshape(n, r, dh), q2, k2, d2, i2.reshape(n, r, dh), go)


def solution(mesh):
    block, decay, state = P("head", "seq", None), P("head", "seq"), P("head", None, None)
    return jax.shard_map(
        functools.partial(local, mesh.shape["seq"], mesh.shape["head"]),
        mesh=mesh,
        in_specs=(block, block, block, decay, state, block, block, decay, state, block),
        out_specs=(block,) * 6,
        check_vma=False,
    )
```

```python
import functools

import jax
import jax.numpy as jnp
from jax import lax
from jax.experimental import pallas as pl
from jax.experimental.pallas import tpu as pltpu
from jax.sharding import PartitionSpec as P

F32 = jnp.float32
BF16 = jnp.bfloat16
VMEM_BYTES = 60 * 1024 * 1024
MESH = pl.DeviceIdType.MESH


def nn(a, b):
    return lax.dot_general(a, b, (((1,), (0,)), ((), ())), preferred_element_type=F32)


def nt(a, b):
    return lax.dot_general(a, b, (((1,), (1,)), ((), ())), preferred_element_type=F32)


def tn(a, b):
    return lax.dot_general(a, b, (((0,), (0,)), ((), ())), preferred_element_type=F32)


def kernel(
    n, hc,
    q1_hbm, k1_hbm, v1_hbm, d1_hbm, i1_hbm, q2_hbm, k2_hbm, d2_hbm, i2_hbm, go_hbm,
    res_hbm, gq1_hbm, gk1_hbm, gv1_hbm, gq2_hbm, gk2_hbm,
    res, gq1, gk1, gv1, gq2, gk2, out_sem,
    q1, k1, v1, d1, i1, q2, k2, d2, i2, go, in_sem,
    dec, mask, wts, ew, tail, part, outs, ks2t, qst, st, v2, gc, cot1, gkp, gvp,
    dt_out, dt_in, sc_out, sc_in, pf_out, pf_in, nm_out, nm_in,
    dt_send, dt_recv, sc_send, sc_recv, pf_send, pf_recv, nm_send, nm_recv,
):
    heads, tok, dh = q1.shape
    per_head = n // heads
    r = dh // per_head
    me, hme = lax.axis_index("seq"), lax.axis_index("head")
    my_head = me // per_head

    def seq_copy(src, dst, send, recv, peer):
        return pltpu.make_async_remote_copy(
            src_ref=src, dst_ref=dst, send_sem=send, recv_sem=recv,
            device_id=(peer, hme), device_id_type=MESH,
        )

    def head_copy(src, dst, send, recv, peer):
        return pltpu.make_async_remote_copy(
            src_ref=src, dst_ref=dst, send_sem=send, recv_sem=recv,
            device_id=(me, peer), device_id_type=MESH,
        )

    def seq_peers(body):
        if n <= 16:
            for step in sorted(range(1, n), key=lambda s: abs(2 * s - n)):
                body(lax.rem(me + step, n))
        else:
            def wrapped(step, carry):
                body(lax.rem(me + step, n))
                return carry
            lax.fori_loop(1, n, wrapped, 0)

    def head_peers(body):
        for step in range(1, hc):
            body(lax.rem(hme + step, hc))

    barrier = pltpu.get_barrier_semaphore()
    seq_peers(lambda p: pl.semaphore_signal(barrier, inc=1, device_id=(p, hme), device_id_type=MESH))
    head_peers(lambda p: pl.semaphore_signal(barrier, inc=1, device_id=(me, p), device_id_type=MESH))

    loads = {}
    order = (
        ("d1", d1_hbm, d1), ("d2", d2_hbm, d2), ("k1", k1_hbm, k1), ("v1", v1_hbm, v1), ("q1", q1_hbm, q1),
        ("i1", i1_hbm.at[me], i1), ("k2", k2_hbm, k2), ("q2", q2_hbm, q2), ("i2", i2_hbm.at[me], i2),
        ("go", go_hbm, go),
    )
    for at, (name, src, dst) in enumerate(order):
        loads[name] = pltpu.make_async_copy(src, dst, in_sem.at[at])
        loads[name].start()

    stores = []

    def emit(src, dst):
        stores.append(pltpu.make_async_copy(src, dst, out_sem.at[len(stores)]))
        stores[-1].start()

    def need(*names):
        for name in names:
            loads[name].wait()

    dec[...] = jnp.zeros_like(dec)
    need("d1", "d2")
    dec[0:heads] = d1[...]
    dec[heads:2 * heads] = d2[...]
    rows_t = lax.broadcasted_iota(jnp.int32, (tok, tok), 0)
    cols_t = lax.broadcasted_iota(jnp.int32, (tok, tok), 1)
    upper = (rows_t <= cols_t).astype(F32).astype(BF16)
    high = dec[...].astype(BF16)
    rest = dec[...] - high.astype(F32)
    middle = rest.astype(BF16)
    low = (rest - middle.astype(F32)).astype(BF16)
    within_row = nn(high, upper) + (nn(middle, upper) + nn(low, upper))
    within_col = within_row.T
    causal = cols_t <= rows_t
    for c in range(2 * heads):
        col = jnp.broadcast_to(within_col[:, c:c + 1], (tok, dh))
        end = jnp.broadcast_to(within_col[tok - 1:tok, c:c + 1], (1, dh))
        ew[c] = jnp.exp(col)
        tail[c] = jnp.exp(end - col)
        dt_out[c:c + 1] = jnp.exp(end)
    dt_in[me] = dt_out[...]

    pl.semaphore_wait(barrier, n - 1 + hc - 1)
    seq_peers(lambda p: seq_copy(dt_out, dt_in.at[me], dt_send, dt_recv.at[me], p).start())

    def scatter(k, states):
        for h in range(heads):
            for a in range(per_head):
                sc_out[k, h * per_head + a] = states[h][a * r:(a + 1) * r]
        seq_peers(lambda p: seq_copy(sc_out.at[k, p], sc_in.at[k, me], sc_send.at[k], sc_recv.at[k, me], p).start())
        sc_in[k, me] = sc_out[k, me]

    def solve(k, first, core, backward):
        seq_peers(lambda p: seq_copy(sc_out.at[k, p], sc_in.at[k, p], sc_send.at[k], sc_recv.at[k, p], p).wait_recv())

        def step(j, carry):
            pf_out[k, j] = carry
            factor = dt_in[j, pl.ds(core * heads + my_head, 1), :]
            return factor * carry + sc_in[k, j]

        if n <= 16:
            carry = first
            for j in (range(n - 1, -1, -1) if backward else range(n)):
                carry = step(j, carry)
        else:
            lax.fori_loop(0, n, lambda s, c: step(n - 1 - s if backward else s, c), first)
        seq_peers(lambda p: seq_copy(pf_out.at[k, p], pf_in.at[k, me], pf_send.at[k], pf_recv.at[k, me], p).start())
        pf_in[k, me] = pf_out[k, me]

    def collect(k):
        seq_peers(lambda p: seq_copy(pf_out.at[k, p], pf_in.at[k, p], pf_send.at[k], pf_recv.at[k, p], p).wait_recv())
        return [
            jnp.concatenate([pf_in[k, h * per_head + a] for a in range(per_head)], axis=0).astype(BF16)
            for h in range(heads)
        ]

    ones = jnp.ones((8, 2 * dh), BF16)

    def row_sum(value):
        high = value.astype(BF16)
        low = (value - high.astype(F32)).astype(BF16)
        return nt(ones, jnp.concatenate([high, low], axis=1))

    def share(m, value):
        nm_out[m] = value
        nm_in[m, hme] = value
        head_peers(lambda p: head_copy(nm_out.at[m], nm_in.at[m, hme], nm_send.at[m], nm_recv.at[m, hme], p).start())

    def shared(m):
        head_peers(lambda p: head_copy(nm_out.at[m], nm_in.at[m, p], nm_send.at[m], nm_recv.at[m, p], p).wait_recv())
        total = nm_in[m, 0]
        for p in range(1, hc):
            total = total + nm_in[m, p]
        return (total * (1.0 / (hc * heads * dh))).T

    def make_weights(c, q, k):
        m = jnp.exp(jnp.where(causal, within_col[:, c:c + 1] - within_row[c:c + 1, :], -1e30))
        mask[c] = m
        wts[c] = (nt(q, k) * m).astype(BF16)

    need("k1", "v1")
    scatter(0, [tn((k1[h].astype(F32) * tail[h]).astype(BF16), v1[h]) for h in range(heads)])
    need("q1")
    for h in range(heads):
        make_weights(h, q1[h], k1[h])
        part[h] = nn(wts[h], v1[h])
    seq_peers(lambda p: seq_copy(dt_out, dt_in.at[p], dt_send, dt_recv.at[p], p).wait_recv())
    need("i1")
    solve(0, i1[...], 0, False)
    need("q2", "k2")
    for h in range(heads):
        make_weights(heads + h, q2[h], k2[h])
    squares = jnp.zeros((tok, dh), F32)
    low = collect(0)
    for h in range(heads):
        st[h] = low[h]
        value = part[h] + ew[h] * nn(q1[h], low[h])
        outs[h] = value
        squares = squares + value * value
    share(0, row_sum(squares))
    for h in range(heads):
        ks2t[h] = (k2[h].astype(F32) * tail[heads + h]).astype(BF16).T
    factor_one = lax.rsqrt(shared(0)[:, 0:1] + 1e-06)

    states = []
    for h in range(heads):
        value = outs[h] * factor_one
        outs[h] = value
        v2[h] = value.astype(BF16)
        states.append(nn(ks2t[h], v2[h]))
    scatter(1, states)
    for h in range(heads):
        part[heads + h] = nn(wts[heads + h], v2[h])
    need("i2")
    solve(1, i2[...], 1, False)
    for h in range(heads):
        qst[h] = (q1[h].astype(F32) * ew[h]).astype(BF16).T
        qst[heads + h] = (q2[h].astype(F32) * ew[heads + h]).astype(BF16).T
    need("go")
    squares = jnp.zeros((tok, dh), F32)
    dots = jnp.zeros((tok, dh), F32)
    low = collect(1)
    for h in range(heads):
        c = heads + h
        st[c] = low[h]
        value = part[c] + ew[c] * nn(q2[h], low[h])
        outs[c] = value
        squares = squares + value * value
        dots = dots + value * go[h].astype(F32)
    first_rows = lax.broadcasted_iota(jnp.int32, (8, tok), 0) < 4
    share(1, jnp.where(first_rows, row_sum(squares), row_sum(dots)))
    both = shared(1)
    factor_two = lax.rsqrt(both[:, 0:1] + 1e-06)
    inner_two = both[:, 4:5] * factor_two

    def backward(core, k, q_ref, k_ref, v_ref, gq_ref, grads):
        states = []
        for h in range(heads):
            gc[h] = grads(h)
            states.append(nn(qst[core * heads + h], gc[h]))
        scatter(k, states)
        scores = []
        for h in range(heads):
            c = core * heads + h
            gvp[h] = tn(wts[c], gc[h])
            scores.append((nt(gc[h], v_ref[h]) * mask[c]).astype(BF16))
        solve(k, jnp.zeros((r, dh), F32), core, True)
        for h in range(heads):
            c = core * heads + h
            gkp[h] = tn(scores[h], q_ref[h])
            gq_ref[h] = (nn(scores[h], k_ref[h]) + ew[c] * nt(gc[h], st[c])).astype(BF16)

    def grads_two(h):
        normalized = outs[heads + h] * factor_two
        res[h] = normalized.astype(BF16)
        return (factor_two * (go[h].astype(F32) - normalized * inner_two)).astype(BF16)

    backward(1, 2, q2, k2, v2, gq2, grads_two)
    emit(res, res_hbm)
    emit(gq2, gq2_hbm)
    dots = jnp.zeros((tok, dh), F32)
    leaving = collect(2)
    for h in range(heads):
        c = heads + h
        cot1[h] = (gvp[h] + tail[c] * nn(k2[h], leaving[h])).astype(BF16)
        dots = dots + cot1[h].astype(F32) * outs[h]
    share(2, row_sum(dots))
    for h in range(heads):
        gk2[h] = (gkp[h] + tail[heads + h] * nt(v2[h], leaving[h])).astype(BF16)
    emit(gk2, gk2_hbm)
    inner_one = shared(2)[:, 0:1]

    def grads_one(h):
        return (factor_one * (cot1[h].astype(F32) - outs[h] * inner_one)).astype(BF16)

    backward(0, 3, q1, k1, v1, gq1, grads_one)
    emit(gq1, gq1_hbm)
    leaving = collect(3)
    for h in range(heads):
        gv1[h] = (gvp[h] + tail[h] * nn(k1[h], leaving[h])).astype(BF16)
    emit(gv1, gv1_hbm)
    for h in range(heads):
        gk1[h] = (gkp[h] + tail[h] * nt(v1[h], leaving[h])).astype(BF16)

    emit(gk1, gk1_hbm)

    def drain(ref, sem, count):
        block = ref.at[pl.ds(0, count)]
        seq_copy(block, block, sem, sem, lax.rem(me + 1, n)).wait_send()

    drain(dt_in, dt_send, n - 1)
    for k in range(4):
        drain(sc_out.at[k], sc_send.at[k], n - 1)
        drain(pf_out.at[k], pf_send.at[k], n - 1)
    for m in range(3):
        drain(nm_in.at[m], nm_send.at[m], hc - 1)
    for copy in stores:
        copy.wait()


def write_out(*refs):
    count = len(refs) // 2
    sems = refs[-1]
    copies = [pltpu.make_async_copy(refs[a], refs[count + a], sems.at[a]) for a in range(count)]
    for copy in copies:
        copy.start()
    for copy in copies:
        copy.wait()


def local(n, hc, q1, k1, v1, d1, i1, q2, k2, d2, i2, go):
    heads, tok, dh = q1.shape
    r = heads * dh // n
    cores = 2 * heads
    pieces = (4, n, r, dh)
    vmem, dma = pltpu.VMEM, pltpu.SemaphoreType.DMA
    block = vmem((heads, tok, dh), BF16)
    decay = vmem((heads, tok), F32)
    piece = vmem((r, dh), F32)
    scratch = [block] * 6 + [dma((6,))] + [
        block, block, block, decay, piece, block, block, decay, piece, block, dma((10,)),
        vmem((8, tok), F32),
        vmem((cores, tok, tok), F32),
        vmem((cores, tok, tok), BF16),
        vmem((cores, tok, dh), F32),
        vmem((cores, tok, dh), F32),
        vmem((cores, tok, dh), F32),
        vmem((cores, tok, dh), F32),
        vmem((heads, dh, tok), BF16),
        vmem((cores, dh, tok), BF16),
        vmem((cores, dh, dh), BF16),
        vmem((heads, tok, dh), BF16),
        vmem((heads, tok, dh), BF16),
        vmem((heads, tok, dh), BF16),
        vmem((heads, tok, dh), F32),
        vmem((heads, tok, dh), F32),
        vmem((8, dh), F32),
        vmem((n, 8, dh), F32),
        vmem(pieces, F32), vmem(pieces, F32), vmem(pieces, F32), vmem(pieces, F32),
        vmem((3, 8, tok), F32),
        vmem((3, hc, 8, tok), F32),
        dma, dma((n,)), dma((4,)), dma((4, n)), dma((4,)), dma((4, n)), dma((3,)), dma((3, hc)),
    ]
    out = jax.ShapeDtypeStruct((heads, tok, dh), BF16)
    results = pl.pallas_call(
        functools.partial(kernel, n, hc),
        out_shape=[out] * 6,
        in_specs=[pl.BlockSpec(memory_space=pltpu.HBM)] * 10,
        out_specs=[pl.BlockSpec(memory_space=pltpu.HBM)] * 6,
        scratch_shapes=scratch,
        compiler_params=pltpu.CompilerParams(
            collective_id=0, has_side_effects=True, vmem_limit_bytes=VMEM_BYTES
        ),
    )(q1, k1, v1, d1, i1.reshape(n, r, dh), q2, k2, d2, i2.reshape(n, r, dh), go)
    return pl.pallas_call(
        write_out,
        out_shape=[out] * 6,
        in_specs=[pl.BlockSpec(memory_space=pltpu.HBM)] * 6,
        out_specs=[pl.BlockSpec(memory_space=pltpu.HBM)] * 6,
        scratch_shapes=[dma((6,))],
        compiler_params=pltpu.CompilerParams(vmem_limit_bytes=VMEM_BYTES),
    )(*results)


def solution(mesh):
    block, decay, state = P("head", "seq", None), P("head", "seq"), P("head", None, None)
    return jax.shard_map(
        functools.partial(local, mesh.shape["seq"], mesh.shape["head"]),
        mesh=mesh,
        in_specs=(block, block, block, decay, state, block, block, decay, state, block),
        out_specs=(block,) * 6,
        check_vma=False,
    )
```

```python
import functools

import jax
import jax.numpy as jnp
from jax import lax
from jax.experimental import pallas as pl
from jax.experimental.pallas import tpu as pltpu
from jax.sharding import PartitionSpec as P

F32 = jnp.float32
BF16 = jnp.bfloat16
VMEM_BYTES = 60 * 1024 * 1024
MESH = pl.DeviceIdType.MESH


def nn(a, b):
    return lax.dot_general(a, b, (((1,), (0,)), ((), ())), preferred_element_type=F32)


def nt(a, b):
    return lax.dot_general(a, b, (((1,), (1,)), ((), ())), preferred_element_type=F32)


def tn(a, b):
    return lax.dot_general(a, b, (((0,), (0,)), ((), ())), preferred_element_type=F32)


def kernel(
    n, hc,
    q1_hbm, k1_hbm, v1_hbm, d1_hbm, i1_hbm, q2_hbm, k2_hbm, d2_hbm, i2_hbm, go_hbm,
    res_hbm, gq1_hbm, gk1_hbm, gv1_hbm, gq2_hbm, gk2_hbm,
    res, gq1, gk1, gv1, gq2, gk2, out_sem,
    q1, k1, v1, d1, i1, q2, k2, d2, i2, go, in_sem,
    dec, mask, wts, ew, tail, part, outs, ks2t, qst, st, v2, gc, cot1, gkp, gvp,
    dt_out, dt_in, sc_out, sc_in, pf_out, pf_in, nm_out, nm_in,
    dt_send, dt_recv, sc_send, sc_recv, pf_send, pf_recv, nm_send, nm_recv,
):
    heads, tok, dh = q1.shape
    r = dh // n
    me, hme = lax.axis_index("seq"), lax.axis_index("head")

    def seq_copy(src, dst, send, recv, peer):
        return pltpu.make_async_remote_copy(
            src_ref=src, dst_ref=dst, send_sem=send, recv_sem=recv,
            device_id=(peer, hme), device_id_type=MESH,
        )

    def head_copy(src, dst, send, recv, peer):
        return pltpu.make_async_remote_copy(
            src_ref=src, dst_ref=dst, send_sem=send, recv_sem=recv,
            device_id=(me, peer), device_id_type=MESH,
        )

    def seq_peers(body):
        if n <= 16:
            for step in sorted(range(1, n), key=lambda s: abs(2 * s - n)):
                body(lax.rem(me + step, n))
        else:
            def wrapped(step, carry):
                body(lax.rem(me + step, n))
                return carry
            lax.fori_loop(1, n, wrapped, 0)

    def head_peers(body):
        for step in range(1, hc):
            body(lax.rem(hme + step, hc))

    barrier = pltpu.get_barrier_semaphore()
    seq_peers(lambda p: pl.semaphore_signal(barrier, inc=1, device_id=(p, hme), device_id_type=MESH))
    head_peers(lambda p: pl.semaphore_signal(barrier, inc=1, device_id=(me, p), device_id_type=MESH))

    loads = {}
    order = (
        ("d1", d1_hbm, d1), ("d2", d2_hbm, d2), ("k1", k1_hbm, k1), ("v1", v1_hbm, v1), ("q1", q1_hbm, q1),
        ("i1", i1_hbm.at[:, me], i1), ("k2", k2_hbm, k2), ("q2", q2_hbm, q2), ("i2", i2_hbm.at[:, me], i2),
        ("go", go_hbm, go),
    )
    for at, (name, src, dst) in enumerate(order):
        loads[name] = pltpu.make_async_copy(src, dst, in_sem.at[at])
        loads[name].start()

    stores = []

    def emit(src, dst):
        stores.append(pltpu.make_async_copy(src, dst, out_sem.at[len(stores)]))
        stores[-1].start()

    def need(*names):
        for name in names:
            loads[name].wait()

    dec[...] = jnp.zeros_like(dec)
    need("d1", "d2")
    dec[0:heads] = d1[...]
    dec[heads:2 * heads] = d2[...]
    rows_t = lax.broadcasted_iota(jnp.int32, (tok, tok), 0)
    cols_t = lax.broadcasted_iota(jnp.int32, (tok, tok), 1)
    upper = (rows_t <= cols_t).astype(F32).astype(BF16)
    high = dec[...].astype(BF16)
    rest = dec[...] - high.astype(F32)
    middle = rest.astype(BF16)
    low = (rest - middle.astype(F32)).astype(BF16)
    within_row = nn(high, upper) + (nn(middle, upper) + nn(low, upper))
    within_col = within_row.T
    causal = cols_t <= rows_t
    for c in range(2 * heads):
        col = jnp.broadcast_to(within_col[:, c:c + 1], (tok, dh))
        end = jnp.broadcast_to(within_col[tok - 1:tok, c:c + 1], (1, dh))
        ew[c] = jnp.exp(col)
        tail[c] = jnp.exp(end - col)
        dt_out[c:c + 1] = jnp.exp(end)
    dt_in[me] = dt_out[...]


    def scatter(k, h, state):
        for p in range(n):
            sc_out[k, h, p] = state[p * r:(p + 1) * r]
        seq_peers(lambda p: seq_copy(
            sc_out.at[k, h, p], sc_in.at[k, h, me], sc_send.at[k, h], sc_recv.at[k, h, me], p).start())
        sc_in[k, h, me] = sc_out[k, h, me]

    def solve(k, h, first, core, backward):
        seq_peers(lambda p: seq_copy(
            sc_out.at[k, h, p], sc_in.at[k, h, p], sc_send.at[k, h], sc_recv.at[k, h, p], p).wait_recv())

        def step(j, carry):
            pf_out[k, h, j] = carry
            return dt_in[j, core * heads + h:core * heads + h + 1, :] * carry + sc_in[k, h, j]

        if n <= 16:
            carry = first
            for j in (range(n - 1, -1, -1) if backward else range(n)):
                carry = step(j, carry)
        else:
            lax.fori_loop(0, n, lambda s, c: step(n - 1 - s if backward else s, c), first)
        seq_peers(lambda p: seq_copy(
            pf_out.at[k, h, p], pf_in.at[k, h, me], pf_send.at[k, h], pf_recv.at[k, h, me], p).start())
        pf_in[k, h, me] = pf_out[k, h, me]

    def collect(k, h):
        seq_peers(lambda p: seq_copy(
            pf_out.at[k, h, p], pf_in.at[k, h, p], pf_send.at[k, h], pf_recv.at[k, h, p], p).wait_recv())
        return jnp.concatenate([pf_in[k, h, p] for p in range(n)], axis=0).astype(BF16)

    ones = jnp.ones((8, 2 * dh), BF16)

    def row_sum(value):
        high = value.astype(BF16)
        low = (value - high.astype(F32)).astype(BF16)
        return nt(ones, jnp.concatenate([high, low], axis=1))

    def share(m, value):
        nm_out[m] = value
        nm_in[m, hme] = value
        head_peers(lambda p: head_copy(nm_out.at[m], nm_in.at[m, hme], nm_send.at[m], nm_recv.at[m, hme], p).start())

    def shared(m):
        head_peers(lambda p: head_copy(nm_out.at[m], nm_in.at[m, p], nm_send.at[m], nm_recv.at[m, p], p).wait_recv())
        total = nm_in[m, 0]
        for p in range(1, hc):
            total = total + nm_in[m, p]
        return (total * (1.0 / (hc * heads * dh))).T

    def make_weights(c, q, k):
        m = jnp.exp(jnp.where(causal, within_col[:, c:c + 1] - within_row[c:c + 1, :], -1e30))
        mask[c] = m
        wts[c] = (nt(q, k) * m).astype(BF16)

    need("k1", "v1")
    states = [tn((k1[h].astype(F32) * tail[h]).astype(BF16), v1[h]) for h in range(heads)]
    pl.semaphore_wait(barrier, n - 1 + hc - 1)
    for h in range(heads):
        scatter(0, h, states[h])
    seq_peers(lambda p: seq_copy(dt_out, dt_in.at[me], dt_send, dt_recv.at[me], p).start())
    need("q1", "i1")
    for h in range(heads):
        make_weights(h, q1[h], k1[h])
        if h == 0:
            seq_peers(lambda p: seq_copy(dt_out, dt_in.at[p], dt_send, dt_recv.at[p], p).wait_recv())
        solve(0, h, i1[h], 0, False)
    for h in range(heads):
        part[h] = nn(wts[h], v1[h])
    need("q2", "k2")
    for h in range(heads):
        make_weights(heads + h, q2[h], k2[h])
    squares = jnp.zeros((tok, dh), F32)
    for h in range(heads):
        st[h] = collect(0, h)
        value = part[h] + ew[h] * nn(q1[h], st[h])
        outs[h] = value
        squares = squares + value * value
    share(0, row_sum(squares))
    for h in range(heads):
        ks2t[h] = (k2[h].astype(F32) * tail[heads + h]).astype(BF16).T
    factor_one = lax.rsqrt(shared(0)[:, 0:1] + 1e-06)

    for h in range(heads):
        value = outs[h] * factor_one
        v2[h] = value.astype(BF16)
        scatter(1, h, nn(ks2t[h], v2[h]))
        outs[h] = value
    need("i2")
    for h in range(heads):
        part[heads + h] = nn(wts[heads + h], v2[h])
        solve(1, h, i2[h], 1, False)
    for h in range(heads):
        qst[h] = (q1[h].astype(F32) * ew[h]).astype(BF16).T
        qst[heads + h] = (q2[h].astype(F32) * ew[heads + h]).astype(BF16).T
    need("go")
    squares = jnp.zeros((tok, dh), F32)
    dots = jnp.zeros((tok, dh), F32)
    for h in range(heads):
        c = heads + h
        st[c] = collect(1, h)
        value = part[c] + ew[c] * nn(q2[h], st[c])
        outs[c] = value
        squares = squares + value * value
        dots = dots + value * go[h].astype(F32)
    first_rows = lax.broadcasted_iota(jnp.int32, (8, tok), 0) < 4
    share(1, jnp.where(first_rows, row_sum(squares), row_sum(dots)))
    both = shared(1)
    factor_two = lax.rsqrt(both[:, 0:1] + 1e-06)
    inner_two = both[:, 4:5] * factor_two

    def backward(core, k, q_ref, k_ref, v_ref, gq_ref, grads):
        for h in range(heads):
            gc[h] = grads(h)
            scatter(k, h, nn(qst[core * heads + h], gc[h]))
        scores = []
        for h in range(heads):
            c = core * heads + h
            gvp[h] = tn(wts[c], gc[h])
            scores.append((nt(gc[h], v_ref[h]) * mask[c]).astype(BF16))
            solve(k, h, jnp.zeros((r, dh), F32), core, True)
        for h in range(heads):
            c = core * heads + h
            gkp[h] = tn(scores[h], q_ref[h])
            gq_ref[h] = (nn(scores[h], k_ref[h]) + ew[c] * nt(gc[h], st[c])).astype(BF16)

    def grads_two(h):
        normalized = outs[heads + h] * factor_two
        res[h] = normalized.astype(BF16)
        return (factor_two * (go[h].astype(F32) - normalized * inner_two)).astype(BF16)

    backward(1, 2, q2, k2, v2, gq2, grads_two)
    emit(res, res_hbm)
    emit(gq2, gq2_hbm)
    dots = jnp.zeros((tok, dh), F32)
    leaving = []
    for h in range(heads):
        c = heads + h
        leaving.append(collect(2, h))
        cot1[h] = (gvp[h] + tail[c] * nn(k2[h], leaving[h])).astype(BF16)
        dots = dots + cot1[h].astype(F32) * outs[h]
    share(2, row_sum(dots))
    for h in range(heads):
        gk2[h] = (gkp[h] + tail[heads + h] * nt(v2[h], leaving[h])).astype(BF16)
    emit(gk2, gk2_hbm)
    inner_one = shared(2)[:, 0:1]

    def grads_one(h):
        return (factor_one * (cot1[h].astype(F32) - outs[h] * inner_one)).astype(BF16)

    backward(0, 3, q1, k1, v1, gq1, grads_one)
    emit(gq1, gq1_hbm)
    for h in range(heads):
        low = collect(3, h)
        gv1[h] = (gvp[h] + tail[h] * nn(k1[h], low)).astype(BF16)
        gk1[h] = (gkp[h] + tail[h] * nt(v1[h], low)).astype(BF16)
    emit(gv1, gv1_hbm)
    emit(gk1, gk1_hbm)

    def drain(ref, sem, count):
        block = ref.at[pl.ds(0, count)]
        seq_copy(block, block, sem, sem, lax.rem(me + 1, n)).wait_send()

    drain(dt_in, dt_send, n - 1)
    for k in range(4):
        for h in range(heads):
            drain(sc_out.at[k, h], sc_send.at[k, h], n - 1)
            drain(pf_out.at[k, h], pf_send.at[k, h], n - 1)
    for m in range(3):
        drain(nm_in.at[m], nm_send.at[m], hc - 1)
    for copy in stores:
        copy.wait()


def write_out(*refs):
    count = (len(refs) - 2) // 3
    loaded, stored = refs[-2:]
    ins, outs, held = (refs[a * count:(a + 1) * count] for a in range(3))
    loads = [pltpu.make_async_copy(ins[a], held[a], loaded.at[a]) for a in range(count)]
    stores = [pltpu.make_async_copy(held[a], outs[a], stored.at[a]) for a in range(count)]
    for load in loads:
        load.start()
    for load, store in zip(loads, stores):
        load.wait()
        store.start()
    for store in stores:
        store.wait()


def local(n, hc, q1, k1, v1, d1, i1, q2, k2, d2, i2, go):
    heads, tok, dh = q1.shape
    r = dh // n
    cores = 2 * heads
    pieces = (4, heads, n, r, dh)
    vmem, dma = pltpu.VMEM, pltpu.SemaphoreType.DMA
    block = vmem((heads, tok, dh), BF16)
    decay = vmem((heads, tok), F32)
    piece = vmem((heads, r, dh), F32)
    scratch = [block] * 6 + [dma((6,))] + [
        block, block, block, decay, piece, block, block, decay, piece, block, dma((10,)),
        vmem((8, tok), F32),
        vmem((cores, tok, tok), F32),
        vmem((cores, tok, tok), BF16),
        vmem((cores, tok, dh), F32),
        vmem((cores, tok, dh), F32),
        vmem((cores, tok, dh), F32),
        vmem((cores, tok, dh), F32),
        vmem((heads, dh, tok), BF16),
        vmem((cores, dh, tok), BF16),
        vmem((cores, dh, dh), BF16),
        vmem((heads, tok, dh), BF16),
        vmem((heads, tok, dh), BF16),
        vmem((heads, tok, dh), BF16),
        vmem((heads, tok, dh), F32),
        vmem((heads, tok, dh), F32),
        vmem((8, dh), F32),
        vmem((n, 8, dh), F32),
        vmem(pieces, F32), vmem(pieces, F32), vmem(pieces, F32), vmem(pieces, F32),
        vmem((3, 8, tok), F32),
        vmem((3, hc, 8, tok), F32),
        dma, dma((n,)), dma((4, heads)), dma((4, heads, n)), dma((4, heads)), dma((4, heads, n)), dma((3,)), dma((3, hc)),
    ]
    out = jax.ShapeDtypeStruct((heads, tok, dh), BF16)
    results = pl.pallas_call(
        functools.partial(kernel, n, hc),
        out_shape=[out] * 6,
        in_specs=[pl.BlockSpec(memory_space=pltpu.HBM)] * 10,
        out_specs=[pl.BlockSpec(memory_space=pltpu.HBM)] * 6,
        scratch_shapes=scratch,
        compiler_params=pltpu.CompilerParams(
            collective_id=0, has_side_effects=True, vmem_limit_bytes=VMEM_BYTES
        ),
    )(q1, k1, v1, d1, i1.reshape(heads, n, r, dh), q2, k2, d2, i2.reshape(heads, n, r, dh), go)
    return pl.pallas_call(
        write_out,
        out_shape=[out] * 6,
        in_specs=[pl.BlockSpec(memory_space=pltpu.HBM)] * 6,
        out_specs=[pl.BlockSpec(memory_space=pltpu.HBM)] * 6,
        scratch_shapes=[block] * 6 + [dma((6,)), dma((6,))],
        compiler_params=pltpu.CompilerParams(vmem_limit_bytes=VMEM_BYTES),
    )(*results)


def solution(mesh):
    block, decay, state = P("head", "seq", None), P("head", "seq"), P("head", None, None)
    return jax.shard_map(
        functools.partial(local, mesh.shape["seq"], mesh.shape["head"]),
        mesh=mesh,
        in_specs=(block, block, block, decay, state, block, block, decay, state, block),
        out_specs=(block,) * 6,
        check_vma=False,
    )
```

```python
import functools

import jax
import jax.numpy as jnp
from jax import lax
from jax.experimental import pallas as pl
from jax.experimental.pallas import tpu as pltpu
from jax.sharding import PartitionSpec as P

F32 = jnp.float32
BF16 = jnp.bfloat16
VMEM_BYTES = 60 * 1024 * 1024
MESH = pl.DeviceIdType.MESH


def nn(a, b):
    return lax.dot_general(a, b, (((1,), (0,)), ((), ())), preferred_element_type=F32)


def nt(a, b):
    return lax.dot_general(a, b, (((1,), (1,)), ((), ())), preferred_element_type=F32)


def tn(a, b):
    return lax.dot_general(a, b, (((0,), (0,)), ((), ())), preferred_element_type=F32)


def kernel(
    n, hc,
    q1_hbm, k1_hbm, v1_hbm, d1_hbm, i1_hbm, q2_hbm, k2_hbm, d2_hbm, i2_hbm, go_hbm,
    res, gq1, gk1, gv1, gq2, gk2,
    q1, k1, v1, d1, i1, q2, k2, d2, i2, go, in_sem,
    dec, mask, wts, ew, tail, part, outs, ks2t, qst, st, v2, gc, cot1, gkp, gvp,
    dt_out, dt_in, sc_out, sc_in, pf_out, pf_in, nm_out, nm_in,
    dt_send, dt_recv, sc_send, sc_recv, pf_send, pf_recv, nm_send, nm_recv,
):
    heads, tok, dh = q1.shape
    r = dh // n
    me, hme = lax.axis_index("seq"), lax.axis_index("head")

    def seq_copy(src, dst, send, recv, peer):
        return pltpu.make_async_remote_copy(
            src_ref=src, dst_ref=dst, send_sem=send, recv_sem=recv,
            device_id=(peer, hme), device_id_type=MESH,
        )

    def head_copy(src, dst, send, recv, peer):
        return pltpu.make_async_remote_copy(
            src_ref=src, dst_ref=dst, send_sem=send, recv_sem=recv,
            device_id=(me, peer), device_id_type=MESH,
        )

    def after(own, step, count):
        return jnp.where(own + step >= count, own + step - count, own + step)

    near = [after(me, step, n) for step in sorted(range(1, n), key=lambda s: abs(2 * s - n))] if n <= 16 else []

    def seq_peers(body):
        if n <= 16:
            for peer in near:
                body(peer)
        else:
            def wrapped(step, carry):
                body(after(me, step, n))
                return carry
            lax.fori_loop(1, n, wrapped, 0)

    head_near = [after(hme, step, hc) for step in range(1, hc)]

    def head_peers(body):
        for peer in head_near:
            body(peer)

    def take(ref, sem, count):
        block = ref.at[pl.ds(0, count)]
        seq_copy(block, block, sem, sem, after(me, 1, n)).wait_recv()

    def drain(ref, sem, count):
        block = ref.at[pl.ds(0, count)]
        seq_copy(block, block, sem, sem, after(me, 1, n)).wait_send()

    barrier = pltpu.get_barrier_semaphore()
    seq_peers(lambda p: pl.semaphore_signal(barrier, inc=1, device_id=(p, hme), device_id_type=MESH))
    head_peers(lambda p: pl.semaphore_signal(barrier, inc=1, device_id=(me, p), device_id_type=MESH))

    loads = {}
    order = (
        ("d1", d1_hbm, d1), ("d2", d2_hbm, d2), ("k1", k1_hbm, k1), ("v1", v1_hbm, v1), ("q1", q1_hbm, q1),
        ("i1", i1_hbm.at[:, me], i1), ("k2", k2_hbm, k2), ("q2", q2_hbm, q2), ("i2", i2_hbm.at[:, me], i2),
        ("go", go_hbm, go),
    )
    for at, (name, src, dst) in enumerate(order):
        loads[name] = pltpu.make_async_copy(src, dst, in_sem.at[at])
        loads[name].start()

    def need(*names):
        for name in names:
            loads[name].wait()

    dec[...] = jnp.zeros_like(dec)
    need("d1", "d2")
    dec[0:heads] = d1[...]
    dec[heads:2 * heads] = d2[...]
    rows_t = lax.broadcasted_iota(jnp.int32, (tok, tok), 0)
    cols_t = lax.broadcasted_iota(jnp.int32, (tok, tok), 1)
    upper = (rows_t <= cols_t).astype(F32).astype(BF16)
    high = dec[...].astype(BF16)
    rest = dec[...] - high.astype(F32)
    middle = rest.astype(BF16)
    low = (rest - middle.astype(F32)).astype(BF16)
    within_row = nn(high, upper) + (nn(middle, upper) + nn(low, upper))
    within_col = within_row.T
    causal = cols_t <= rows_t

    def make_decay(c):
        col = jnp.broadcast_to(within_col[:, c:c + 1], (tok, dh))
        end = jnp.broadcast_to(within_col[tok - 1:tok, c:c + 1], (1, dh))
        ew[c] = jnp.exp(col)
        tail[c] = jnp.exp(end - col)
        dt_out[c:c + 1] = jnp.exp(end)

    for c in range(heads):
        make_decay(c)


    def scatter(k, h, state):
        for p in range(n):
            sc_out[k, h, p] = state[p * r:(p + 1) * r]
        seq_peers(lambda p: seq_copy(
            sc_out.at[k, h, p], sc_in.at[k, h, me], sc_send.at[k, h], sc_recv.at[k, h], p).start())
        sc_in[k, h, me] = sc_out[k, h, me]

    def solve(k, h, first, core, backward):
        take(sc_in.at[k, h], sc_recv.at[k, h], n - 1)

        def step(j, carry):
            pf_out[k, h, j] = carry
            return dt_in[j, core * heads + h:core * heads + h + 1, :] * carry + sc_in[k, h, j]

        if n <= 16:
            carry = first
            for j in (range(n - 1, -1, -1) if backward else range(n)):
                carry = step(j, carry)
        else:
            lax.fori_loop(0, n, lambda s, c: step(n - 1 - s if backward else s, c), first)
        seq_peers(lambda p: seq_copy(
            pf_out.at[k, h, p], pf_in.at[k, h, me], pf_send.at[k, h], pf_recv.at[k, h], p).start())
        pf_in[k, h, me] = pf_out[k, h, me]

    def collect(k, h):
        take(pf_in.at[k, h], pf_recv.at[k, h], n - 1)
        return jnp.concatenate([pf_in[k, h, p] for p in range(n)], axis=0).astype(BF16)

    ones = jnp.ones((8, 2 * dh), BF16)

    def row_sum(value):
        high = value.astype(BF16)
        low = (value - high.astype(F32)).astype(BF16)
        return nt(ones, jnp.concatenate([high, low], axis=1))

    def share(m, value):
        nm_out[m] = value
        nm_in[m, hme] = value
        head_peers(lambda p: head_copy(nm_out.at[m], nm_in.at[m, hme], nm_send.at[m], nm_recv.at[m], p).start())

    def shared(m):
        take(nm_in.at[m], nm_recv.at[m], hc - 1)
        total = nm_in[m, 0]
        for p in range(1, hc):
            total = total + nm_in[m, p]
        return (total * (1.0 / (hc * heads * dh))).T

    def make_weights(c, q, k):
        m = jnp.exp(jnp.where(causal, within_col[:, c:c + 1] - within_row[c:c + 1, :], -1e30))
        mask[c] = m
        wts[c] = (nt(q, k) * m).astype(BF16)

    need("k1", "v1")
    states = [tn((k1[h].astype(F32) * tail[h]).astype(BF16), v1[h]) for h in range(heads)]
    pl.semaphore_wait(barrier, n - 1 + hc - 1)
    for h in range(heads):
        scatter(0, h, states[h])
    for c in range(heads, 2 * heads):
        make_decay(c)
    dt_in[me] = dt_out[...]
    seq_peers(lambda p: seq_copy(dt_out, dt_in.at[me], dt_send, dt_recv, p).start())
    need("q1", "i1")
    for h in range(heads):
        make_weights(h, q1[h], k1[h])
        if h == 0:
            take(dt_in, dt_recv, n - 1)
        solve(0, h, i1[h], 0, False)
    for h in range(heads):
        part[h] = nn(wts[h], v1[h])
    need("q2", "k2")
    for h in range(heads):
        make_weights(heads + h, q2[h], k2[h])
    squares = jnp.zeros((tok, dh), F32)
    for h in range(heads):
        st[h] = collect(0, h)
        value = part[h] + ew[h] * nn(q1[h], st[h])
        outs[h] = value
        squares = squares + value * value
    share(0, row_sum(squares))
    for h in range(heads):
        ks2t[h] = (k2[h].astype(F32) * tail[heads + h]).astype(BF16).T
    factor_one = lax.rsqrt(shared(0)[:, 0:1] + 1e-06)

    for h in range(heads):
        value = outs[h] * factor_one
        v2[h] = value.astype(BF16)
        scatter(1, h, nn(ks2t[h], v2[h]))
        outs[h] = value
    need("i2")
    for h in range(heads):
        part[heads + h] = nn(wts[heads + h], v2[h])
        solve(1, h, i2[h], 1, False)
    for h in range(heads):
        qst[h] = (q1[h].astype(F32) * ew[h]).astype(BF16).T
        qst[heads + h] = (q2[h].astype(F32) * ew[heads + h]).astype(BF16).T
    need("go")
    squares = jnp.zeros((tok, dh), F32)
    dots = jnp.zeros((tok, dh), F32)
    for h in range(heads):
        c = heads + h
        st[c] = collect(1, h)
        value = part[c] + ew[c] * nn(q2[h], st[c])
        outs[c] = value
        squares = squares + value * value
        dots = dots + value * go[h].astype(F32)
    first_rows = lax.broadcasted_iota(jnp.int32, (8, tok), 0) < 4
    share(1, jnp.where(first_rows, row_sum(squares), row_sum(dots)))
    both = shared(1)
    factor_two = lax.rsqrt(both[:, 0:1] + 1e-06)
    inner_two = both[:, 4:5] * factor_two

    def backward(core, k, q_ref, k_ref, v_ref, gq_ref, grads):
        for h in range(heads):
            gc[h] = grads(h)
            scatter(k, h, nn(qst[core * heads + h], gc[h]))
        scores = []
        for h in range(heads):
            c = core * heads + h
            gvp[h] = tn(wts[c], gc[h])
            scores.append((nt(gc[h], v_ref[h]) * mask[c]).astype(BF16))
            solve(k, h, jnp.zeros((r, dh), F32), core, True)
        for h in range(heads):
            c = core * heads + h
            gkp[h] = tn(scores[h], q_ref[h])
            gq_ref[h] = (nn(scores[h], k_ref[h]) + ew[c] * nt(gc[h], st[c])).astype(BF16)

    def grads_two(h):
        normalized = outs[heads + h] * factor_two
        res[h] = normalized.astype(BF16)
        return (factor_two * (go[h].astype(F32) - normalized * inner_two)).astype(BF16)

    backward(1, 2, q2, k2, v2, gq2, grads_two)
    dots = jnp.zeros((tok, dh), F32)
    leaving = []
    for h in range(heads):
        c = heads + h
        leaving.append(collect(2, h))
        cot1[h] = (gvp[h] + tail[c] * nn(k2[h], leaving[h])).astype(BF16)
        dots = dots + cot1[h].astype(F32) * outs[h]
    share(2, row_sum(dots))
    for h in range(heads):
        gk2[h] = (gkp[h] + tail[heads + h] * nt(v2[h], leaving[h])).astype(BF16)
    inner_one = shared(2)[:, 0:1]

    def grads_one(h):
        return (factor_one * (cot1[h].astype(F32) - outs[h] * inner_one)).astype(BF16)

    backward(0, 3, q1, k1, v1, gq1, grads_one)
    for h in range(heads):
        low = collect(3, h)
        gv1[h] = (gvp[h] + tail[h] * nn(k1[h], low)).astype(BF16)
        gk1[h] = (gkp[h] + tail[h] * nt(v1[h], low)).astype(BF16)

    drain(dt_in, dt_send, n - 1)
    for k in range(4):
        for h in range(heads):
            drain(sc_out.at[k, h], sc_send.at[k, h], n - 1)
            drain(pf_out.at[k, h], pf_send.at[k, h], n - 1)
    for m in range(3):
        drain(nm_in.at[m], nm_send.at[m], hc - 1)


def write_out(*refs):
    count = len(refs) // 2
    sems = refs[-1]
    copies = [pltpu.make_async_copy(refs[a], refs[count + a], sems.at[a]) for a in range(count)]
    for copy in copies:
        copy.start()
    for copy in copies:
        copy.wait()


def local(n, hc, q1, k1, v1, d1, i1, q2, k2, d2, i2, go):
    heads, tok, dh = q1.shape
    r = dh // n
    cores = 2 * heads
    pieces = (4, heads, n, r, dh)
    vmem, dma = pltpu.VMEM, pltpu.SemaphoreType.DMA
    block = vmem((heads, tok, dh), BF16)
    decay = vmem((heads, tok), F32)
    piece = vmem((heads, r, dh), F32)
    scratch = [
        block, block, block, decay, piece, block, block, decay, piece, block, dma((10,)),
        vmem((8, tok), F32),
        vmem((cores, tok, tok), F32),
        vmem((cores, tok, tok), BF16),
        vmem((cores, tok, dh), F32),
        vmem((cores, tok, dh), F32),
        vmem((cores, tok, dh), F32),
        vmem((cores, tok, dh), F32),
        vmem((heads, dh, tok), BF16),
        vmem((cores, dh, tok), BF16),
        vmem((cores, dh, dh), BF16),
        vmem((heads, tok, dh), BF16),
        vmem((heads, tok, dh), BF16),
        vmem((heads, tok, dh), BF16),
        vmem((heads, tok, dh), F32),
        vmem((heads, tok, dh), F32),
        vmem((8, dh), F32),
        vmem((n, 8, dh), F32),
        vmem(pieces, F32), vmem(pieces, F32), vmem(pieces, F32), vmem(pieces, F32),
        vmem((3, 8, tok), F32),
        vmem((3, hc, 8, tok), F32),
        dma, dma, dma((4, heads)), dma((4, heads)), dma((4, heads)), dma((4, heads)), dma((3,)), dma((3,)),
    ]
    out = jax.ShapeDtypeStruct((heads, tok, dh), BF16)
    results = pl.pallas_call(
        functools.partial(kernel, n, hc),
        out_shape=[pltpu.VMEM(out.shape, out.dtype)] * 6,
        in_specs=[pl.BlockSpec(memory_space=pltpu.HBM)] * 10,
        out_specs=[pl.BlockSpec(memory_space=pltpu.VMEM)] * 6,
        scratch_shapes=scratch,
        compiler_params=pltpu.CompilerParams(
            collective_id=0, has_side_effects=True, vmem_limit_bytes=VMEM_BYTES
        ),
    )(q1, k1, v1, d1, i1.reshape(heads, n, r, dh), q2, k2, d2, i2.reshape(heads, n, r, dh), go)
    return pl.pallas_call(
        write_out,
        out_shape=[out] * 6,
        in_specs=[pl.BlockSpec(memory_space=pltpu.VMEM)] * 6,
        out_specs=[pl.BlockSpec(memory_space=pltpu.HBM)] * 6,
        scratch_shapes=[dma((6,))],
        compiler_params=pltpu.CompilerParams(vmem_limit_bytes=4 * 1024 * 1024),
    )(*results)


def solution(mesh):
    block, decay, state = P("head", "seq", None), P("head", "seq"), P("head", None, None)
    return jax.shard_map(
        functools.partial(local, mesh.shape["seq"], mesh.shape["head"]),
        mesh=mesh,
        in_specs=(block, block, block, decay, state, block, block, decay, state, block),
        out_specs=(block,) * 6,
        check_vma=False,
    )
```

```python
import functools

import jax
import jax.numpy as jnp
from jax import lax
from jax.experimental import pallas as pl
from jax.experimental.pallas import tpu as pltpu
from jax.sharding import PartitionSpec as P

F32 = jnp.float32
BF16 = jnp.bfloat16
VMEM_BYTES = 60 * 1024 * 1024
MESH = pl.DeviceIdType.MESH


def nn(a, b):
    return lax.dot_general(a, b, (((1,), (0,)), ((), ())), preferred_element_type=F32)


def nt(a, b):
    return lax.dot_general(a, b, (((1,), (1,)), ((), ())), preferred_element_type=F32)


def tn(a, b):
    return lax.dot_general(a, b, (((0,), (0,)), ((), ())), preferred_element_type=F32)


def kernel(
    n, hc,
    q1_hbm, k1_hbm, v1_hbm, d1_hbm, i1_hbm, q2_hbm, k2_hbm, d2_hbm, i2_hbm, go_hbm,
    res, gq1, gk1, gv1, gq2, gk2,
    q1, k1, v1, d1, i1, q2, k2, d2, i2, go, in_sem,
    dec, mask, wts, ew, tail, part, outs, ks2t, qst, st, v2, gc, cot1, gkp, gvp,
    dt_out, dt_in, sc_out, sc_in, pf_out, pf_in, tt_out, tt_in, nm_out, nm_in,
    dt_send, dt_recv, sc_send, sc_recv, pf_send, pf_recv, tt_send, tt_recv, nm_send, nm_recv,
):
    heads, tok, dh = q1.shape
    g = n // 2
    r = dh // g
    me, hme = lax.axis_index("seq"), lax.axis_index("head")

    def seq_copy(src, dst, send, recv, peer):
        return pltpu.make_async_remote_copy(
            src_ref=src, dst_ref=dst, send_sem=send, recv_sem=recv,
            device_id=(peer, hme), device_id_type=MESH,
        )

    def head_copy(src, dst, send, recv, peer):
        return pltpu.make_async_remote_copy(
            src_ref=src, dst_ref=dst, send_sem=send, recv_sem=recv,
            device_id=(me, peer), device_id_type=MESH,
        )

    def after(own, step, count):
        return jnp.where(own + step >= count, own + step - count, own + step)

    low_half = me < g
    base = jnp.where(low_half, 0, g)
    w = me - base
    other = jnp.where(low_half, me + g, me - g)
    near = [after(w, step, g) for step in sorted(range(1, g), key=lambda s: abs(2 * s - g))] if g <= 16 else []

    def seq_peers(body):
        if g <= 16:
            for peer in near:
                body(peer)
        else:
            def wrapped(step, carry):
                body(after(w, step, g))
                return carry
            lax.fori_loop(1, g, wrapped, 0)

    head_near = [after(hme, step, hc) for step in range(1, hc)]

    def head_peers(body):
        for peer in head_near:
            body(peer)

    def take(ref, sem, count):
        block = ref.at[pl.ds(0, count)]
        seq_copy(block, block, sem, sem, other).wait_recv()

    def drain(ref, sem, count):
        block = ref.at[pl.ds(0, count)]
        seq_copy(block, block, sem, sem, other).wait_send()

    barrier = pltpu.get_barrier_semaphore()
    seq_peers(lambda p: pl.semaphore_signal(barrier, inc=1, device_id=(base + p, hme), device_id_type=MESH))
    pl.semaphore_signal(barrier, inc=1, device_id=(other, hme), device_id_type=MESH)
    head_peers(lambda p: pl.semaphore_signal(barrier, inc=1, device_id=(me, p), device_id_type=MESH))

    loads = {}
    order = (
        ("d1", d1_hbm, d1), ("d2", d2_hbm, d2), ("k1", k1_hbm, k1), ("v1", v1_hbm, v1), ("q1", q1_hbm, q1),
        ("i1", i1_hbm.at[:, w], i1), ("k2", k2_hbm, k2), ("q2", q2_hbm, q2), ("i2", i2_hbm.at[:, w], i2),
        ("go", go_hbm, go),
    )
    for at, (name, src, dst) in enumerate(order):
        loads[name] = pltpu.make_async_copy(src, dst, in_sem.at[at])
        loads[name].start()

    def need(*names):
        for name in names:
            loads[name].wait()

    dec[...] = jnp.zeros_like(dec)
    need("d1", "d2")
    dec[0:heads] = d1[...]
    dec[heads:2 * heads] = d2[...]
    rows_t = lax.broadcasted_iota(jnp.int32, (tok, tok), 0)
    cols_t = lax.broadcasted_iota(jnp.int32, (tok, tok), 1)
    upper = (rows_t <= cols_t).astype(F32).astype(BF16)
    high = dec[...].astype(BF16)
    rest = dec[...] - high.astype(F32)
    middle = rest.astype(BF16)
    low = (rest - middle.astype(F32)).astype(BF16)
    within_row = nn(high, upper) + (nn(middle, upper) + nn(low, upper))
    within_col = within_row.T
    causal = cols_t <= rows_t

    def make_decay(c):
        col = jnp.broadcast_to(within_col[:, c:c + 1], (tok, dh))
        end = jnp.broadcast_to(within_col[tok - 1:tok, c:c + 1], (1, dh))
        ew[c] = jnp.exp(col)
        tail[c] = jnp.exp(end - col)
        dt_out[c:c + 1] = jnp.exp(end)

    for c in range(heads):
        make_decay(c)


    def scatter(k, h, state):
        for p in range(g):
            sc_out[k, h, p] = state[p * r:(p + 1) * r]
        seq_peers(lambda p: seq_copy(
            sc_out.at[k, h, p], sc_in.at[k, h, w], sc_send.at[k, h], sc_recv.at[k, h], base + p).start())
        sc_in[k, h, w] = sc_out[k, h, w]

    def total_copy(k, h):
        return seq_copy(tt_out.at[k, h], tt_in.at[k, h], tt_send.at[k, h], tt_recv.at[k, h], other)

    def leads(backward):
        return jnp.logical_not(low_half) if backward else low_half

    def solve(k, h, first, core, backward):
        take(sc_in.at[k, h], sc_recv.at[k, h], g - 1)

        @pl.when(leads(backward))
        def _():
            tt_in[k, h] = first

        @pl.when(leads(not backward))
        def _():
            total_copy(k, h).wait_recv()

        def step(j, carry):
            pf_out[k, h, j] = carry
            return dt_in[j, core * heads + h:core * heads + h + 1, :] * carry + sc_in[k, h, j]

        carry = tt_in[k, h]
        if g <= 16:
            for j in (range(g - 1, -1, -1) if backward else range(g)):
                carry = step(j, carry)
        else:
            carry = lax.fori_loop(0, g, lambda s, c: step(g - 1 - s if backward else s, c), carry)
        tt_out[k, h] = carry

        @pl.when(leads(backward))
        def _():
            total_copy(k, h).start()

        seq_peers(lambda p: seq_copy(
            pf_out.at[k, h, p], pf_in.at[k, h, w], pf_send.at[k, h], pf_recv.at[k, h], base + p).start())
        pf_in[k, h, w] = pf_out[k, h, w]

    def collect(k, h):
        take(pf_in.at[k, h], pf_recv.at[k, h], g - 1)
        return jnp.concatenate([pf_in[k, h, p] for p in range(g)], axis=0).astype(BF16)

    ones = jnp.ones((8, 2 * dh), BF16)

    def row_sum(value):
        high = value.astype(BF16)
        low = (value - high.astype(F32)).astype(BF16)
        return nt(ones, jnp.concatenate([high, low], axis=1))

    def share(m, value):
        nm_out[m] = value
        nm_in[m, hme] = value
        head_peers(lambda p: head_copy(nm_out.at[m], nm_in.at[m, hme], nm_send.at[m], nm_recv.at[m], p).start())

    def shared(m):
        take(nm_in.at[m], nm_recv.at[m], hc - 1)
        total = nm_in[m, 0]
        for p in range(1, hc):
            total = total + nm_in[m, p]
        return (total * (1.0 / (hc * heads * dh))).T

    def make_weights(c, q, k):
        m = jnp.exp(jnp.where(causal, within_col[:, c:c + 1] - within_row[c:c + 1, :], -1e30))
        mask[c] = m
        wts[c] = (nt(q, k) * m).astype(BF16)

    need("k1", "v1")
    states = [tn((k1[h].astype(F32) * tail[h]).astype(BF16), v1[h]) for h in range(heads)]
    pl.semaphore_wait(barrier, g + hc - 1)
    for h in range(heads):
        scatter(0, h, states[h])
    for c in range(heads, 2 * heads):
        make_decay(c)
    dt_in[w] = dt_out[...]
    seq_peers(lambda p: seq_copy(dt_out, dt_in.at[w], dt_send, dt_recv, base + p).start())
    need("q1", "i1")
    for h in range(heads):
        make_weights(h, q1[h], k1[h])
        if h == 0:
            take(dt_in, dt_recv, g - 1)
        solve(0, h, i1[h], 0, False)
    for h in range(heads):
        part[h] = nn(wts[h], v1[h])
    need("q2", "k2")
    for h in range(heads):
        make_weights(heads + h, q2[h], k2[h])
    squares = jnp.zeros((tok, dh), F32)
    for h in range(heads):
        st[h] = collect(0, h)
        value = part[h] + ew[h] * nn(q1[h], st[h])
        outs[h] = value
        squares = squares + value * value
    share(0, row_sum(squares))
    for h in range(heads):
        ks2t[h] = (k2[h].astype(F32) * tail[heads + h]).astype(BF16).T
    factor_one = lax.rsqrt(shared(0)[:, 0:1] + 1e-06)

    for h in range(heads):
        value = outs[h] * factor_one
        v2[h] = value.astype(BF16)
        scatter(1, h, nn(ks2t[h], v2[h]))
        outs[h] = value
    need("i2")
    for h in range(heads):
        part[heads + h] = nn(wts[heads + h], v2[h])
        solve(1, h, i2[h], 1, False)
    for h in range(heads):
        qst[h] = (q1[h].astype(F32) * ew[h]).astype(BF16).T
        qst[heads + h] = (q2[h].astype(F32) * ew[heads + h]).astype(BF16).T
    need("go")
    squares = jnp.zeros((tok, dh), F32)
    dots = jnp.zeros((tok, dh), F32)
    for h in range(heads):
        c = heads + h
        st[c] = collect(1, h)
        value = part[c] + ew[c] * nn(q2[h], st[c])
        outs[c] = value
        squares = squares + value * value
        dots = dots + value * go[h].astype(F32)
    first_rows = lax.broadcasted_iota(jnp.int32, (8, tok), 0) < 4
    share(1, jnp.where(first_rows, row_sum(squares), row_sum(dots)))
    both = shared(1)
    factor_two = lax.rsqrt(both[:, 0:1] + 1e-06)
    inner_two = both[:, 4:5] * factor_two

    def backward(core, k, q_ref, k_ref, v_ref, gq_ref, grads):
        for h in range(heads):
            gc[h] = grads(h)
            scatter(k, h, nn(qst[core * heads + h], gc[h]))
        scores = []
        for h in range(heads):
            c = core * heads + h
            gvp[h] = tn(wts[c], gc[h])
            scores.append((nt(gc[h], v_ref[h]) * mask[c]).astype(BF16))
            solve(k, h, jnp.zeros((r, dh), F32), core, True)
        for h in range(heads):
            c = core * heads + h
            gkp[h] = tn(scores[h], q_ref[h])
            gq_ref[h] = (nn(scores[h], k_ref[h]) + ew[c] * nt(gc[h], st[c])).astype(BF16)

    def grads_two(h):
        normalized = outs[heads + h] * factor_two
        res[h] = normalized.astype(BF16)
        return (factor_two * (go[h].astype(F32) - normalized * inner_two)).astype(BF16)

    backward(1, 2, q2, k2, v2, gq2, grads_two)
    dots = jnp.zeros((tok, dh), F32)
    leaving = []
    for h in range(heads):
        c = heads + h
        leaving.append(collect(2, h))
        cot1[h] = (gvp[h] + tail[c] * nn(k2[h], leaving[h])).astype(BF16)
        dots = dots + cot1[h].astype(F32) * outs[h]
    share(2, row_sum(dots))
    for h in range(heads):
        gk2[h] = (gkp[h] + tail[heads + h] * nt(v2[h], leaving[h])).astype(BF16)
    inner_one = shared(2)[:, 0:1]

    def grads_one(h):
        return (factor_one * (cot1[h].astype(F32) - outs[h] * inner_one)).astype(BF16)

    backward(0, 3, q1, k1, v1, gq1, grads_one)
    for h in range(heads):
        low = collect(3, h)
        gv1[h] = (gvp[h] + tail[h] * nn(k1[h], low)).astype(BF16)
        gk1[h] = (gkp[h] + tail[h] * nt(v1[h], low)).astype(BF16)

    drain(dt_in, dt_send, g - 1)
    for k in range(4):
        for h in range(heads):
            drain(sc_out.at[k, h], sc_send.at[k, h], g - 1)
            drain(pf_out.at[k, h], pf_send.at[k, h], g - 1)

            @pl.when(leads(k >= 2))
            def _():
                total_copy(k, h).wait_send()

    for m in range(3):
        drain(nm_in.at[m], nm_send.at[m], hc - 1)


def write_out(*refs):
    count = len(refs) // 2
    sems = refs[-1]
    copies = [pltpu.make_async_copy(refs[a], refs[count + a], sems.at[a]) for a in range(count)]
    for copy in copies:
        copy.start()
    for copy in copies:
        copy.wait()


def local(n, hc, q1, k1, v1, d1, i1, q2, k2, d2, i2, go):
    heads, tok, dh = q1.shape
    g = n // 2
    r = dh // g
    cores = 2 * heads
    pieces = (4, heads, g, r, dh)
    vmem, dma = pltpu.VMEM, pltpu.SemaphoreType.DMA
    block = vmem((heads, tok, dh), BF16)
    decay = vmem((heads, tok), F32)
    piece = vmem((heads, r, dh), F32)
    scratch = [
        block, block, block, decay, piece, block, block, decay, piece, block, dma((10,)),
        vmem((8, tok), F32),
        vmem((cores, tok, tok), F32),
        vmem((cores, tok, tok), BF16),
        vmem((cores, tok, dh), F32),
        vmem((cores, tok, dh), F32),
        vmem((cores, tok, dh), F32),
        vmem((cores, tok, dh), F32),
        vmem((heads, dh, tok), BF16),
        vmem((cores, dh, tok), BF16),
        vmem((cores, dh, dh), BF16),
        vmem((heads, tok, dh), BF16),
        vmem((heads, tok, dh), BF16),
        vmem((heads, tok, dh), BF16),
        vmem((heads, tok, dh), F32),
        vmem((heads, tok, dh), F32),
        vmem((8, dh), F32),
        vmem((g, 8, dh), F32),
        vmem(pieces, F32), vmem(pieces, F32), vmem(pieces, F32), vmem(pieces, F32),
        vmem((4, heads, r, dh), F32), vmem((4, heads, r, dh), F32),
        vmem((3, 8, tok), F32),
        vmem((3, hc, 8, tok), F32),
        dma, dma, dma((4, heads)), dma((4, heads)), dma((4, heads)), dma((4, heads)), dma((4, heads)), dma((4, heads)),
        dma((3,)), dma((3,)),
    ]
    out = jax.ShapeDtypeStruct((heads, tok, dh), BF16)
    results = pl.pallas_call(
        functools.partial(kernel, n, hc),
        out_shape=[pltpu.VMEM(out.shape, out.dtype)] * 6,
        in_specs=[pl.BlockSpec(memory_space=pltpu.HBM)] * 10,
        out_specs=[pl.BlockSpec(memory_space=pltpu.VMEM)] * 6,
        scratch_shapes=scratch,
        compiler_params=pltpu.CompilerParams(
            collective_id=0, has_side_effects=True, vmem_limit_bytes=VMEM_BYTES
        ),
    )(q1, k1, v1, d1, i1.reshape(heads, g, r, dh), q2, k2, d2, i2.reshape(heads, g, r, dh), go)
    return pl.pallas_call(
        write_out,
        out_shape=[out] * 6,
        in_specs=[pl.BlockSpec(memory_space=pltpu.VMEM)] * 6,
        out_specs=[pl.BlockSpec(memory_space=pltpu.HBM)] * 6,
        scratch_shapes=[dma((6,))],
        compiler_params=pltpu.CompilerParams(vmem_limit_bytes=4 * 1024 * 1024),
    )(*results)


def solution(mesh):
    block, decay, state = P("head", "seq", None), P("head", "seq"), P("head", None, None)
    return jax.shard_map(
        functools.partial(local, mesh.shape["seq"], mesh.shape["head"]),
        mesh=mesh,
        in_specs=(block, block, block, decay, state, block, block, decay, state, block),
        out_specs=(block,) * 6,
        check_vma=False,
    )
```

```python
import functools

import jax
import jax.numpy as jnp
from jax import lax
from jax.experimental import pallas as pl
from jax.experimental.pallas import tpu as pltpu
from jax.sharding import PartitionSpec as P

F32 = jnp.float32
BF16 = jnp.bfloat16
VMEM_BYTES = 60 * 1024 * 1024
MESH = pl.DeviceIdType.MESH


def nn(a, b):
    return lax.dot_general(a, b, (((1,), (0,)), ((), ())), preferred_element_type=F32)


def nt(a, b):
    return lax.dot_general(a, b, (((1,), (1,)), ((), ())), preferred_element_type=F32)


def tn(a, b):
    return lax.dot_general(a, b, (((0,), (0,)), ((), ())), preferred_element_type=F32)


def kernel(
    n, hc,
    q1_hbm, k1_hbm, v1_hbm, d1_hbm, i1_hbm, q2_hbm, k2_hbm, d2_hbm, i2_hbm, go_hbm,
    res, gq1, gk1, gv1, gq2, gk2,
    q1, k1, v1, d1, i1, q2, k2, d2, i2, go, in_sem,
    dec, mask, wts, ew, tail, part, outs, ks2t, qst, st, v2, gc, cot1, gkp, gvp,
    dt_out, dt_in, sc_out, sc_in, pf_out, pf_in, tt_out, tt_in, nm_out, nm_in,
    dt_send, dt_recv, sc_send, sc_recv, pf_send, pf_recv, tt_send, tt_recv, nm_send, nm_recv,
):
    heads, tok, dh = q1.shape
    g = n // 2
    r = dh // g
    me, hme = lax.axis_index("seq"), lax.axis_index("head")

    def seq_copy(src, dst, send, recv, peer):
        return pltpu.make_async_remote_copy(
            src_ref=src, dst_ref=dst, send_sem=send, recv_sem=recv,
            device_id=(peer, hme), device_id_type=MESH,
        )

    def head_copy(src, dst, send, recv, peer):
        return pltpu.make_async_remote_copy(
            src_ref=src, dst_ref=dst, send_sem=send, recv_sem=recv,
            device_id=(me, peer), device_id_type=MESH,
        )

    def after(own, step, count):
        return jnp.where(own + step >= count, own + step - count, own + step)

    low_half = me < g
    base = jnp.where(low_half, 0, g)
    w = me - base
    other = jnp.where(low_half, me + g, me - g)
    near = [after(w, step, g) for step in sorted(range(1, g), key=lambda s: abs(2 * s - g))] if g <= 16 else []

    def seq_peers(body):
        if g <= 16:
            for peer in near:
                body(peer)
        else:
            def wrapped(step, carry):
                body(after(w, step, g))
                return carry
            lax.fori_loop(1, g, wrapped, 0)

    head_near = [after(hme, step, hc) for step in range(1, hc)]

    def head_peers(body):
        for peer in head_near:
            body(peer)

    def take(ref, sem, count):
        block = ref.at[pl.ds(0, count)]
        seq_copy(block, block, sem, sem, other).wait_recv()

    def drain(ref, sem, count):
        block = ref.at[pl.ds(0, count)]
        seq_copy(block, block, sem, sem, other).wait_send()

    barrier = pltpu.get_barrier_semaphore()
    seq_peers(lambda p: pl.semaphore_signal(barrier, inc=1, device_id=(base + p, hme), device_id_type=MESH))
    pl.semaphore_signal(barrier, inc=1, device_id=(other, hme), device_id_type=MESH)
    head_peers(lambda p: pl.semaphore_signal(barrier, inc=1, device_id=(me, p), device_id_type=MESH))

    loads = {}
    order = (
        ("d1", d1_hbm, d1), ("d2", d2_hbm, d2), ("k1", k1_hbm, k1), ("v1", v1_hbm, v1), ("q1", q1_hbm, q1),
        ("i1", i1_hbm.at[:, w], i1), ("k2", k2_hbm, k2), ("q2", q2_hbm, q2), ("i2", i2_hbm.at[:, w], i2),
        ("go", go_hbm, go),
    )
    for at, (name, src, dst) in enumerate(order):
        loads[name] = pltpu.make_async_copy(src, dst, in_sem.at[at])
        loads[name].start()

    def need(*names):
        for name in names:
            loads[name].wait()

    def scatter(k, h, state):
        for p in range(g):
            sc_out[k, h, p] = state[p * r:(p + 1) * r]
        seq_peers(lambda p: seq_copy(
            sc_out.at[k, h, p], sc_in.at[k, h, w], sc_send.at[k, h], sc_recv.at[k, h], base + p).start())
        sc_in[k, h, w] = sc_out[k, h, w]

    def total_copy(k, h):
        return seq_copy(tt_out.at[k, h], tt_in.at[k, h], tt_send.at[k, h], tt_recv.at[k, h], other)

    def leads(backward):
        return jnp.logical_not(low_half) if backward else low_half

    def solve(k, h, first, core, backward):
        take(sc_in.at[k, h], sc_recv.at[k, h], g - 1)

        @pl.when(leads(backward))
        def _():
            tt_in[k, h] = first

        @pl.when(leads(not backward))
        def _():
            total_copy(k, h).wait_recv()

        def step(j, carry):
            pf_out[k, h, j] = carry
            return dt_in[j, core * heads + h:core * heads + h + 1, :] * carry + sc_in[k, h, j]

        carry = tt_in[k, h]
        if g <= 16:
            for j in (range(g - 1, -1, -1) if backward else range(g)):
                carry = step(j, carry)
        else:
            carry = lax.fori_loop(0, g, lambda s, c: step(g - 1 - s if backward else s, c), carry)
        tt_out[k, h] = carry

        @pl.when(leads(backward))
        def _():
            total_copy(k, h).start()

        seq_peers(lambda p: seq_copy(
            pf_out.at[k, h, p], pf_in.at[k, h, w], pf_send.at[k, h], pf_recv.at[k, h], base + p).start())
        pf_in[k, h, w] = pf_out[k, h, w]

    def collect(k, h):
        take(pf_in.at[k, h], pf_recv.at[k, h], g - 1)
        return jnp.concatenate([pf_in[k, h, p] for p in range(g)], axis=0).astype(BF16)

    dec[...] = jnp.zeros_like(dec)
    need("d1", "d2")
    dec[0:heads] = d1[...]
    dec[heads:2 * heads] = d2[...]
    rows_t = lax.broadcasted_iota(jnp.int32, (tok, tok), 0)
    cols_t = lax.broadcasted_iota(jnp.int32, (tok, tok), 1)
    upper = (rows_t <= cols_t).astype(F32).astype(BF16)
    high = dec[...].astype(BF16)
    rest = dec[...] - high.astype(F32)
    middle = rest.astype(BF16)
    low = (rest - middle.astype(F32)).astype(BF16)
    within_row = nn(high, upper) + (nn(middle, upper) + nn(low, upper))
    end_row = jnp.broadcast_to(within_row[:, tok - 1:tok], within_row.shape)
    tail_row = jnp.exp(end_row - within_row)
    ew_row = jnp.exp(within_row)
    dt_out[...] = jnp.exp(end_row[:, 0:dh])

    def scaled_t(block, row, c):
        return (block.T.astype(F32) * row[c:c + 1, :]).astype(BF16)

    need("k1", "v1")
    states = [nn(scaled_t(k1[h], tail_row, h), v1[h]) for h in range(heads)]
    pl.semaphore_wait(barrier, g + hc - 1)
    for h in range(heads):
        scatter(0, h, states[h])
    dt_in[w] = dt_out[...]
    seq_peers(lambda p: seq_copy(dt_out, dt_in.at[w], dt_send, dt_recv, base + p).start())

    within_col = within_row.T
    causal = cols_t <= rows_t

    def make_decay(c):
        col = jnp.broadcast_to(within_col[:, c:c + 1], (tok, dh))
        end = jnp.broadcast_to(within_col[tok - 1:tok, c:c + 1], (1, dh))
        ew[c] = jnp.exp(col)
        tail[c] = jnp.exp(end - col)

    for c in range(heads):
        make_decay(c)


    ones = jnp.ones((8, 2 * dh), BF16)

    def row_sum(value):
        high = value.astype(BF16)
        low = (value - high.astype(F32)).astype(BF16)
        return nt(ones, jnp.concatenate([high, low], axis=1))

    def share(m, value):
        nm_out[m] = value
        nm_in[m, hme] = value
        head_peers(lambda p: head_copy(nm_out.at[m], nm_in.at[m, hme], nm_send.at[m], nm_recv.at[m], p).start())

    def shared(m):
        take(nm_in.at[m], nm_recv.at[m], hc - 1)
        total = nm_in[m, 0]
        for p in range(1, hc):
            total = total + nm_in[m, p]
        return total * (1.0 / (hc * heads * dh))

    def make_weights(c, q, k):
        m = jnp.exp(jnp.where(causal, within_col[:, c:c + 1] - within_row[c:c + 1, :], -1e30))
        mask[c] = m
        wts[c] = (nt(q, k) * m).astype(BF16)

    need("q1", "i1")
    for h in range(heads):
        make_weights(h, q1[h], k1[h])
    take(dt_in, dt_recv, g - 1)
    for h in range(heads):
        solve(0, h, i1[h], 0, False)
    for h in range(heads):
        part[h] = nn(wts[h], v1[h])
        make_decay(heads + h)
    need("q2", "k2")
    for h in range(heads):
        make_weights(heads + h, q2[h], k2[h])
    squares = jnp.zeros((tok, dh), F32)
    for h in range(heads):
        st[h] = collect(0, h)
        value = part[h] + ew[h] * nn(q1[h], st[h])
        outs[h] = value
        squares = squares + value * value
    share(0, row_sum(squares))
    for h in range(heads):
        ks2t[h] = scaled_t(k2[h], tail_row, heads + h)
    factor_one = lax.rsqrt(shared(0) + 1e-06).T[:, 0:1]

    for h in range(heads):
        value = outs[h] * factor_one
        v2[h] = value.astype(BF16)
        scatter(1, h, nn(ks2t[h], v2[h]))
        outs[h] = value
    need("i2")
    for h in range(heads):
        part[heads + h] = nn(wts[heads + h], v2[h])
    for h in range(heads):
        solve(1, h, i2[h], 1, False)
    for h in range(heads):
        qst[h] = scaled_t(q1[h], ew_row, h)
        qst[heads + h] = scaled_t(q2[h], ew_row, heads + h)
    need("go")
    squares = jnp.zeros((tok, dh), F32)
    dots = jnp.zeros((tok, dh), F32)
    for h in range(heads):
        c = heads + h
        st[c] = collect(1, h)
        value = part[c] + ew[c] * nn(q2[h], st[c])
        outs[c] = value
        squares = squares + value * value
        dots = dots + value * go[h].astype(F32)
    first_rows = lax.broadcasted_iota(jnp.int32, (8, tok), 0) < 4
    share(1, jnp.where(first_rows, row_sum(squares), row_sum(dots)))
    both = shared(1)
    factor_row = lax.rsqrt(both[0:1] + 1e-06)
    both = jnp.where(first_rows, factor_row, factor_row * both[4:5]).T
    factor_two, inner_two = both[:, 0:1], both[:, 4:5]

    def backward(core, k, q_ref, k_ref, v_ref, gq_ref, grads):
        for h in range(heads):
            gc[h] = grads(h)
            scatter(k, h, nn(qst[core * heads + h], gc[h]))
        scores = []
        for h in range(heads):
            c = core * heads + h
            gvp[h] = tn(wts[c], gc[h])
            scores.append((nt(gc[h], v_ref[h]) * mask[c]).astype(BF16))
        for h in range(heads):
            solve(k, h, jnp.zeros((r, dh), F32), core, True)
        for h in range(heads):
            c = core * heads + h
            gkp[h] = tn(scores[h], q_ref[h])
            gq_ref[h] = (nn(scores[h], k_ref[h]) + ew[c] * nt(gc[h], st[c])).astype(BF16)

    def grads_two(h):
        normalized = outs[heads + h] * factor_two
        res[h] = normalized.astype(BF16)
        return (factor_two * (go[h].astype(F32) - normalized * inner_two)).astype(BF16)

    backward(1, 2, q2, k2, v2, gq2, grads_two)
    dots = jnp.zeros((tok, dh), F32)
    leaving = []
    for h in range(heads):
        c = heads + h
        leaving.append(collect(2, h))
        cot1[h] = (gvp[h] + tail[c] * nn(k2[h], leaving[h])).astype(BF16)
        dots = dots + cot1[h].astype(F32) * outs[h]
    share(2, row_sum(dots))
    for h in range(heads):
        gk2[h] = (gkp[h] + tail[heads + h] * nt(v2[h], leaving[h])).astype(BF16)
    inner_one = shared(2).T[:, 0:1]

    def grads_one(h):
        return (factor_one * (cot1[h].astype(F32) - outs[h] * inner_one)).astype(BF16)

    backward(0, 3, q1, k1, v1, gq1, grads_one)
    for h in range(heads):
        low = collect(3, h)
        gv1[h] = (gvp[h] + tail[h] * nn(k1[h], low)).astype(BF16)
        gk1[h] = (gkp[h] + tail[h] * nt(v1[h], low)).astype(BF16)

    drain(dt_in, dt_send, g - 1)
    for k in range(4):
        for h in range(heads):
            drain(sc_out.at[k, h], sc_send.at[k, h], g - 1)
            drain(pf_out.at[k, h], pf_send.at[k, h], g - 1)

            @pl.when(leads(k >= 2))
            def _():
                total_copy(k, h).wait_send()

    for m in range(3):
        drain(nm_in.at[m], nm_send.at[m], hc - 1)


def write_out(*refs):
    count = len(refs) // 2
    sems = refs[-1]
    copies = [pltpu.make_async_copy(refs[a], refs[count + a], sems.at[a]) for a in range(count)]
    for copy in copies:
        copy.start()
    for copy in copies:
        copy.wait()


def local(n, hc, q1, k1, v1, d1, i1, q2, k2, d2, i2, go):
    heads, tok, dh = q1.shape
    g = n // 2
    r = dh // g
    cores = 2 * heads
    pieces = (4, heads, g, r, dh)
    vmem, dma = pltpu.VMEM, pltpu.SemaphoreType.DMA
    block = vmem((heads, tok, dh), BF16)
    decay = vmem((heads, tok), F32)
    piece = vmem((heads, r, dh), F32)
    scratch = [
        block, block, block, decay, piece, block, block, decay, piece, block, dma((10,)),
        vmem((8, tok), F32),
        vmem((cores, tok, tok), F32),
        vmem((cores, tok, tok), BF16),
        vmem((cores, tok, dh), F32),
        vmem((cores, tok, dh), F32),
        vmem((cores, tok, dh), F32),
        vmem((cores, tok, dh), F32),
        vmem((heads, dh, tok), BF16),
        vmem((cores, dh, tok), BF16),
        vmem((cores, dh, dh), BF16),
        vmem((heads, tok, dh), BF16),
        vmem((heads, tok, dh), BF16),
        vmem((heads, tok, dh), BF16),
        vmem((heads, tok, dh), F32),
        vmem((heads, tok, dh), F32),
        vmem((8, dh), F32),
        vmem((g, 8, dh), F32),
        vmem(pieces, F32), vmem(pieces, F32), vmem(pieces, F32), vmem(pieces, F32),
        vmem((4, heads, r, dh), F32), vmem((4, heads, r, dh), F32),
        vmem((3, 8, tok), F32),
        vmem((3, hc, 8, tok), F32),
        dma, dma, dma((4, heads)), dma((4, heads)), dma((4, heads)), dma((4, heads)), dma((4, heads)), dma((4, heads)),
        dma((3,)), dma((3,)),
    ]
    out = jax.ShapeDtypeStruct((heads, tok, dh), BF16)
    results = pl.pallas_call(
        functools.partial(kernel, n, hc),
        out_shape=[pltpu.VMEM(out.shape, out.dtype)] * 6,
        in_specs=[pl.BlockSpec(memory_space=pltpu.HBM)] * 10,
        out_specs=[pl.BlockSpec(memory_space=pltpu.VMEM)] * 6,
        scratch_shapes=scratch,
        compiler_params=pltpu.CompilerParams(
            collective_id=0, has_side_effects=True, vmem_limit_bytes=VMEM_BYTES
        ),
    )(q1, k1, v1, d1, i1.reshape(heads, g, r, dh), q2, k2, d2, i2.reshape(heads, g, r, dh), go)
    return pl.pallas_call(
        write_out,
        out_shape=[out] * 6,
        in_specs=[pl.BlockSpec(memory_space=pltpu.VMEM)] * 6,
        out_specs=[pl.BlockSpec(memory_space=pltpu.HBM)] * 6,
        scratch_shapes=[dma((6,))],
        compiler_params=pltpu.CompilerParams(vmem_limit_bytes=4 * 1024 * 1024),
    )(*results)


def solution(mesh):
    block, decay, state = P("head", "seq", None), P("head", "seq"), P("head", None, None)
    return jax.shard_map(
        functools.partial(local, mesh.shape["seq"], mesh.shape["head"]),
        mesh=mesh,
        in_specs=(block, block, block, decay, state, block, block, decay, state, block),
        out_specs=(block,) * 6,
        check_vma=False,
    )
```

```python
import functools

import jax
import jax.numpy as jnp
from jax import lax
from jax.experimental import pallas as pl
from jax.experimental.pallas import tpu as pltpu
from jax.sharding import PartitionSpec as P

F32 = jnp.float32
BF16 = jnp.bfloat16
VMEM_BYTES = 60 * 1024 * 1024
MESH = pl.DeviceIdType.MESH


def nn(a, b):
    return lax.dot_general(a, b, (((1,), (0,)), ((), ())), preferred_element_type=F32)


def nt(a, b):
    return lax.dot_general(a, b, (((1,), (1,)), ((), ())), preferred_element_type=F32)


def tn(a, b):
    return lax.dot_general(a, b, (((0,), (0,)), ((), ())), preferred_element_type=F32)


def kernel(
    n, hc,
    q1_hbm, k1_hbm, v1_hbm, d1_hbm, i1_hbm, q2_hbm, k2_hbm, d2_hbm, i2_hbm, go_hbm,
    res, gq1, gk1, gv1, gq2, gk2,
    q1, k1, v1, d1, i1, q2, k2, d2, i2, go, in_sem,
    dec, mask, scores, wts, ew, tail, part, outs, ks2t, qst, st, v2, gc, cot1, gkp, gvp,
    dt_out, dt_in, sc_out, sc_in, pf_out, pf_in, tt_out, tt_in, nm_out, nm_in,
    dt_send, dt_recv, sc_send, sc_recv, pf_send, pf_recv, tt_send, tt_recv, nm_send, nm_recv,
):
    heads, tok, dh = q1.shape
    g = n // 2
    r = dh // g
    me, hme = lax.axis_index("seq"), lax.axis_index("head")

    def seq_copy(src, dst, send, recv, peer):
        return pltpu.make_async_remote_copy(
            src_ref=src, dst_ref=dst, send_sem=send, recv_sem=recv,
            device_id=(peer, hme), device_id_type=MESH,
        )

    def head_copy(src, dst, send, recv, peer):
        return pltpu.make_async_remote_copy(
            src_ref=src, dst_ref=dst, send_sem=send, recv_sem=recv,
            device_id=(me, peer), device_id_type=MESH,
        )

    def after(own, step, count):
        return jnp.where(own + step >= count, own + step - count, own + step)

    low_half = me < g
    base = jnp.where(low_half, 0, g)
    w = me - base
    other = jnp.where(low_half, me + g, me - g)
    near = [after(w, step, g) for step in sorted(range(1, g), key=lambda s: abs(2 * s - g))] if g <= 16 else []

    def seq_peers(body):
        if g <= 16:
            for peer in near:
                body(peer)
        else:
            def wrapped(step, carry):
                body(after(w, step, g))
                return carry
            lax.fori_loop(1, g, wrapped, 0)

    head_near = [after(hme, step, hc) for step in range(1, hc)]

    def head_peers(body):
        for peer in head_near:
            body(peer)

    def take(ref, sem, count):
        block = ref.at[pl.ds(0, count)]
        seq_copy(block, block, sem, sem, other).wait_recv()

    def drain(ref, sem, count):
        block = ref.at[pl.ds(0, count)]
        seq_copy(block, block, sem, sem, other).wait_send()

    barrier = pltpu.get_barrier_semaphore()
    seq_peers(lambda p: pl.semaphore_signal(barrier, inc=1, device_id=(base + p, hme), device_id_type=MESH))
    pl.semaphore_signal(barrier, inc=1, device_id=(other, hme), device_id_type=MESH)
    head_peers(lambda p: pl.semaphore_signal(barrier, inc=1, device_id=(me, p), device_id_type=MESH))

    loads = {}
    order = (
        ("d1", d1_hbm, d1), ("d2", d2_hbm, d2), ("k1", k1_hbm, k1), ("v1", v1_hbm, v1), ("q1", q1_hbm, q1),
        ("i1", i1_hbm.at[:, w], i1), ("k2", k2_hbm, k2), ("q2", q2_hbm, q2), ("i2", i2_hbm.at[:, w], i2),
        ("go", go_hbm, go),
    )
    for at, (name, src, dst) in enumerate(order):
        loads[name] = pltpu.make_async_copy(src, dst, in_sem.at[at])
        loads[name].start()

    def need(*names):
        for name in names:
            loads[name].wait()

    def scatter(k, h, state):
        for p in range(g):
            sc_out[k, h, p] = state[p * r:(p + 1) * r]
        seq_peers(lambda p: seq_copy(
            sc_out.at[k, h, p], sc_in.at[k, h, w], sc_send.at[k, h], sc_recv.at[k, h], base + p).start())
        sc_in[k, h, w] = sc_out[k, h, w]

    def total_copy(k, h):
        return seq_copy(tt_out.at[k, h], tt_in.at[k, h], tt_send.at[k, h], tt_recv.at[k, h], other)

    def leads(backward):
        return jnp.logical_not(low_half) if backward else low_half

    def solve(k, h, first, core, backward):
        take(sc_in.at[k, h], sc_recv.at[k, h], g - 1)

        @pl.when(leads(backward))
        def _():
            tt_in[k, h] = first

        @pl.when(leads(not backward))
        def _():
            total_copy(k, h).wait_recv()

        def step(j, carry):
            pf_out[k, h, j] = carry
            return dt_in[j, core * heads + h:core * heads + h + 1, :] * carry + sc_in[k, h, j]

        carry = tt_in[k, h]
        if g <= 16:
            for j in (range(g - 1, -1, -1) if backward else range(g)):
                carry = step(j, carry)
        else:
            carry = lax.fori_loop(0, g, lambda s, c: step(g - 1 - s if backward else s, c), carry)
        tt_out[k, h] = carry

        @pl.when(leads(backward))
        def _():
            total_copy(k, h).start()

        seq_peers(lambda p: seq_copy(
            pf_out.at[k, h, p], pf_in.at[k, h, w], pf_send.at[k, h], pf_recv.at[k, h], base + p).start())
        pf_in[k, h, w] = pf_out[k, h, w]

    def solve_beside(k, firsts, core, backward, beside):
        pl.when(leads(not backward))(beside)
        for h in range(heads):
            solve(k, h, firsts[h], core, backward)
        pl.when(leads(backward))(beside)

    def collect(k, h):
        take(pf_in.at[k, h], pf_recv.at[k, h], g - 1)
        return jnp.concatenate([pf_in[k, h, p] for p in range(g)], axis=0).astype(BF16)

    dec[...] = jnp.zeros_like(dec)
    need("d1", "d2")
    dec[0:heads] = d1[...]
    dec[heads:2 * heads] = d2[...]
    rows_t = lax.broadcasted_iota(jnp.int32, (tok, tok), 0)
    cols_t = lax.broadcasted_iota(jnp.int32, (tok, tok), 1)
    upper = (rows_t <= cols_t).astype(F32).astype(BF16)
    high = dec[...].astype(BF16)
    rest = dec[...] - high.astype(F32)
    middle = rest.astype(BF16)
    low = (rest - middle.astype(F32)).astype(BF16)
    within_row = nn(high, upper) + (nn(middle, upper) + nn(low, upper))
    end_row = jnp.broadcast_to(within_row[:, tok - 1:tok], within_row.shape)
    tail_row = jnp.exp(end_row - within_row)
    ew_row = jnp.exp(within_row)
    dt_out[...] = jnp.exp(end_row[:, 0:dh])

    def scaled_t(block, row, c):
        return (block.T.astype(F32) * row[c:c + 1, :]).astype(BF16)

    need("k1", "v1")
    states = [nn(scaled_t(k1[h], tail_row, h), v1[h]) for h in range(heads)]
    pl.semaphore_wait(barrier, g + hc - 1)
    for h in range(heads):
        scatter(0, h, states[h])
    dt_in[w] = dt_out[...]
    seq_peers(lambda p: seq_copy(dt_out, dt_in.at[w], dt_send, dt_recv, base + p).start())

    within_col = within_row.T
    causal = cols_t <= rows_t

    def make_decay(c):
        col = jnp.broadcast_to(within_col[:, c:c + 1], (tok, dh))
        end = jnp.broadcast_to(within_col[tok - 1:tok, c:c + 1], (1, dh))
        ew[c] = jnp.exp(col)
        tail[c] = jnp.exp(end - col)

    for c in range(heads):
        make_decay(c)


    ones = jnp.ones((8, 2 * dh), BF16)

    def row_sum(value):
        high = value.astype(BF16)
        low = (value - high.astype(F32)).astype(BF16)
        return nt(ones, jnp.concatenate([high, low], axis=1))

    def share(m, value):
        nm_out[m] = value
        nm_in[m, hme] = value
        head_peers(lambda p: head_copy(nm_out.at[m], nm_in.at[m, hme], nm_send.at[m], nm_recv.at[m], p).start())

    def shared(m):
        take(nm_in.at[m], nm_recv.at[m], hc - 1)
        total = nm_in[m, 0]
        for p in range(1, hc):
            total = total + nm_in[m, p]
        return total * (1.0 / (hc * heads * dh))

    def make_weights(c, q, k):
        m = jnp.exp(jnp.where(causal, within_col[:, c:c + 1] - within_row[c:c + 1, :], -1e30))
        mask[c] = m
        wts[c] = (nt(q, k) * m).astype(BF16)

    need("q1", "i1")
    for h in range(heads):
        make_weights(h, q1[h], k1[h])
    take(dt_in, dt_recv, g - 1)
    need("q2", "k2")

    def beside():
        for h in range(heads):
            part[h] = nn(wts[h], v1[h])
            make_decay(heads + h)
            make_weights(heads + h, q2[h], k2[h])

    solve_beside(0, [i1[h] for h in range(heads)], 0, False, beside)
    squares = jnp.zeros((tok, dh), F32)
    for h in range(heads):
        st[h] = collect(0, h)
        value = part[h] + ew[h] * nn(q1[h], st[h])
        outs[h] = value
        squares = squares + value * value
    share(0, row_sum(squares))
    for h in range(heads):
        ks2t[h] = scaled_t(k2[h], tail_row, heads + h)
    factor_one = lax.rsqrt(shared(0) + 1e-06).T[:, 0:1]

    for h in range(heads):
        value = outs[h] * factor_one
        v2[h] = value.astype(BF16)
        scatter(1, h, nn(ks2t[h], v2[h]))
        outs[h] = value
    need("i2")
    for h in range(heads):
        part[heads + h] = nn(wts[heads + h], v2[h])

    def beside():
        for h in range(heads):
            qst[h] = scaled_t(q1[h], ew_row, h)
            qst[heads + h] = scaled_t(q2[h], ew_row, heads + h)

    solve_beside(1, [i2[h] for h in range(heads)], 1, False, beside)
    need("go")
    squares = jnp.zeros((tok, dh), F32)
    dots = jnp.zeros((tok, dh), F32)
    for h in range(heads):
        c = heads + h
        st[c] = collect(1, h)
        value = part[c] + ew[c] * nn(q2[h], st[c])
        outs[c] = value
        squares = squares + value * value
        dots = dots + value * go[h].astype(F32)
    first_rows = lax.broadcasted_iota(jnp.int32, (8, tok), 0) < 4
    share(1, jnp.where(first_rows, row_sum(squares), row_sum(dots)))
    both = shared(1)
    factor_row = lax.rsqrt(both[0:1] + 1e-06)
    both = jnp.where(first_rows, factor_row, factor_row * both[4:5]).T
    factor_two, inner_two = both[:, 0:1], both[:, 4:5]

    def backward(core, k, q_ref, k_ref, v_ref, gq_ref, grads):
        for h in range(heads):
            gc[h] = grads(h)
            scatter(k, h, nn(qst[core * heads + h], gc[h]))
        for h in range(heads):
            c = core * heads + h
            gvp[h] = tn(wts[c], gc[h])
            scores[h] = (nt(gc[h], v_ref[h]) * mask[c]).astype(BF16)

        def beside():
            for h in range(heads):
                c = core * heads + h
                gkp[h] = tn(scores[h], q_ref[h])
                gq_ref[h] = (nn(scores[h], k_ref[h]) + ew[c] * nt(gc[h], st[c])).astype(BF16)

        solve_beside(k, [jnp.zeros((r, dh), F32)] * heads, core, True, beside)

    def grads_two(h):
        normalized = outs[heads + h] * factor_two
        res[h] = normalized.astype(BF16)
        return (factor_two * (go[h].astype(F32) - normalized * inner_two)).astype(BF16)

    backward(1, 2, q2, k2, v2, gq2, grads_two)
    dots = jnp.zeros((tok, dh), F32)
    leaving = []
    for h in range(heads):
        c = heads + h
        leaving.append(collect(2, h))
        cot1[h] = (gvp[h] + tail[c] * nn(k2[h], leaving[h])).astype(BF16)
        dots = dots + cot1[h].astype(F32) * outs[h]
    share(2, row_sum(dots))
    for h in range(heads):
        gk2[h] = (gkp[h] + tail[heads + h] * nt(v2[h], leaving[h])).astype(BF16)
    inner_one = shared(2).T[:, 0:1]

    def grads_one(h):
        return (factor_one * (cot1[h].astype(F32) - outs[h] * inner_one)).astype(BF16)

    backward(0, 3, q1, k1, v1, gq1, grads_one)
    for h in range(heads):
        low = collect(3, h)
        gv1[h] = (gvp[h] + tail[h] * nn(k1[h], low)).astype(BF16)
        gk1[h] = (gkp[h] + tail[h] * nt(v1[h], low)).astype(BF16)

    drain(dt_in, dt_send, g - 1)
    for k in range(4):
        for h in range(heads):
            drain(sc_out.at[k, h], sc_send.at[k, h], g - 1)
            drain(pf_out.at[k, h], pf_send.at[k, h], g - 1)

            @pl.when(leads(k >= 2))
            def _():
                total_copy(k, h).wait_send()

    for m in range(3):
        drain(nm_in.at[m], nm_send.at[m], hc - 1)


def write_out(*refs):
    count = len(refs) // 2
    sems = refs[-1]
    copies = [pltpu.make_async_copy(refs[a], refs[count + a], sems.at[a]) for a in range(count)]
    for copy in copies:
        copy.start()
    for copy in copies:
        copy.wait()


def local(n, hc, q1, k1, v1, d1, i1, q2, k2, d2, i2, go):
    heads, tok, dh = q1.shape
    g = n // 2
    r = dh // g
    cores = 2 * heads
    pieces = (4, heads, g, r, dh)
    vmem, dma = pltpu.VMEM, pltpu.SemaphoreType.DMA
    block = vmem((heads, tok, dh), BF16)
    decay = vmem((heads, tok), F32)
    piece = vmem((heads, r, dh), F32)
    scratch = [
        block, block, block, decay, piece, block, block, decay, piece, block, dma((10,)),
        vmem((8, tok), F32),
        vmem((cores, tok, tok), F32),
        vmem((heads, tok, tok), BF16),
        vmem((cores, tok, tok), BF16),
        vmem((cores, tok, dh), F32),
        vmem((cores, tok, dh), F32),
        vmem((cores, tok, dh), F32),
        vmem((cores, tok, dh), F32),
        vmem((heads, dh, tok), BF16),
        vmem((cores, dh, tok), BF16),
        vmem((cores, dh, dh), BF16),
        vmem((heads, tok, dh), BF16),
        vmem((heads, tok, dh), BF16),
        vmem((heads, tok, dh), BF16),
        vmem((heads, tok, dh), F32),
        vmem((heads, tok, dh), F32),
        vmem((8, dh), F32),
        vmem((g, 8, dh), F32),
        vmem(pieces, F32), vmem(pieces, F32), vmem(pieces, F32), vmem(pieces, F32),
        vmem((4, heads, r, dh), F32), vmem((4, heads, r, dh), F32),
        vmem((3, 8, tok), F32),
        vmem((3, hc, 8, tok), F32),
        dma, dma, dma((4, heads)), dma((4, heads)), dma((4, heads)), dma((4, heads)), dma((4, heads)), dma((4, heads)),
        dma((3,)), dma((3,)),
    ]
    out = jax.ShapeDtypeStruct((heads, tok, dh), BF16)
    results = pl.pallas_call(
        functools.partial(kernel, n, hc),
        out_shape=[pltpu.VMEM(out.shape, out.dtype)] * 6,
        in_specs=[pl.BlockSpec(memory_space=pltpu.HBM)] * 10,
        out_specs=[pl.BlockSpec(memory_space=pltpu.VMEM)] * 6,
        scratch_shapes=scratch,
        compiler_params=pltpu.CompilerParams(
            collective_id=0, has_side_effects=True, vmem_limit_bytes=VMEM_BYTES
        ),
    )(q1, k1, v1, d1, i1.reshape(heads, g, r, dh), q2, k2, d2, i2.reshape(heads, g, r, dh), go)
    return pl.pallas_call(
        write_out,
        out_shape=[out] * 6,
        in_specs=[pl.BlockSpec(memory_space=pltpu.VMEM)] * 6,
        out_specs=[pl.BlockSpec(memory_space=pltpu.HBM)] * 6,
        scratch_shapes=[dma((6,))],
        compiler_params=pltpu.CompilerParams(vmem_limit_bytes=4 * 1024 * 1024),
    )(*results)


def solution(mesh):
    block, decay, state = P("head", "seq", None), P("head", "seq"), P("head", None, None)
    return jax.shard_map(
        functools.partial(local, mesh.shape["seq"], mesh.shape["head"]),
        mesh=mesh,
        in_specs=(block, block, block, decay, state, block, block, decay, state, block),
        out_specs=(block,) * 6,
        check_vma=False,
    )
```
